1024 devices in a mesh: row: 32 (over x, z_lo), col: 32 (over z_hi, y, core).
Axes of the slice: x: 8, y: 8, z: 8 (z_hi: 2, z_lo: 4; z = z_hi * 4 + z_lo), core: 2. Of those that a mesh axis runs over, the one named last changes fastest.
Arguments:
- left_blocks: bfloat16 [128, 4096, 128], P('row', 'col'), may hold values from -6 to 6
- right_blocks: bfloat16 [64, 4096, 128], P('col', 'row'), may hold values from -0.078125 to 0.078125
- pair_lists: int32 [1024, 256, 3], P(('row', 'col')), may hold values from 0 to 3, as said below
- pair_count: int32 [1024, 32], P(('row', 'col')), may hold values from 1 to 8, as said below
Outputs:
- product_blocks: bfloat16 [2048, 128, 128], P(('row', 'col'))
The draws below stay inside these ranges and needn't reach their ends.
Inputs may be any that keep to these rules, and one draw needn't show every extreme that they name: `pair_lists`: Columns: a stored left block below 4, a stored right block below 2, a stored product block below 2; the live slots of one list are distinct triples. `pair_count`: live slots per list; some list is full.
All inputs are finite; a program needn't handle non-finite values.
Results may differ from the reference program's by a relative error of at most 0.001.
Values may be sent and summed in bfloat16 or wider, within the bound.
No kernel may reach another device: no remote copies, remote signals or barrier semaphores. Data moves between devices by JAX's collectives and lax.ppermute only.
A program may use at most 32 MiB of HBM per device.

```python
import jax
import jax.numpy as jnp
from jax import lax

BS = 128
NA = 4
NB = 2
NC = 2
NT = 8
N_ROW = 32
N_COL = 32


def draw_pair_lists(key, part):
    key = jax.random.fold_in(key, 3)
    total = NA * NB * NC
    scores = jax.random.randint(key, (N_ROW * N_ROW, N_COL, total), 0, 1 << 20) * total
    scores = scores + jnp.arange(total, dtype=jnp.int32)
    scores = scores.at[0, 0, (NA - 1) * NB * NC].set(-1)
    order = jnp.argsort(scores, axis=-1)[..., :NT].astype(jnp.int32)
    stacked = jnp.stack([order // (NB * NC), order // NC % NB, order % NC], axis=-1)
    return stacked.reshape(N_ROW * N_ROW, N_COL * NT, 3).astype(jnp.int32)


def draw_pair_count(key, part):
    key = jax.random.fold_in(key, 7)
    first_key, second_key = jax.random.split(key)
    level = jax.random.randint(first_key, (N_ROW, 1, N_COL), 2, NT + 1)
    level = level.at[0, 0, 0].set(NT)
    fraction = jax.random.randint(second_key, (N_ROW, N_ROW, N_COL), 0, 1 << 16)
    counts = 1 + fraction * level // 65536
    counts = jnp.minimum(counts, level)
    counts = counts.at[:, 0, :].set(level[:, 0, :])
    return counts.reshape(N_ROW * N_ROW, N_COL).astype(jnp.int32)


def steps_of(key, dims, cuts, least, top_value):
    def one(dim, shards_of):
        draws = jax.random.uniform(jax.random.fold_in(jax.random.fold_in(key, 6), dim), (shards_of,), jnp.float32, least / len(cuts), top_value / len(cuts))
        return jnp.repeat(jnp.exp(draws), dims[dim] // shards_of).reshape((-1,) + (1,) * (len(dims) - dim - 1))

    loudness = one(*cuts[0])
    for cut in cuts[1:]:
        loudness = loudness * one(*cut)
    return loudness


def centred(own_key, extent, spread, most, cuts=(), kind=jnp.bfloat16):
    entries = spread * jax.random.normal(own_key, extent, jnp.float32)
    if cuts:
        entries = entries * steps_of(own_key, extent, cuts, -0.22, 0.18)
    return jnp.clip(entries, -most, most).astype(kind)


def setup_inputs(seed: int = 0) -> dict:
    arg_keys = jax.random.split(jax.random.key(seed), 5)
    left_blocks = centred(arg_keys[0], (N_ROW * NA, N_COL * BS, BS), 1.0, 6.0, ((0, 32), (1, 32)))
    right_blocks = centred(arg_keys[1], (N_COL * NB, N_ROW * BS, BS), (BS * N_COL * (NT + 4) // (4 * NC)) ** -0.5, 0.078125, ((0, 32), (1, 32)))
    pair_lists = draw_pair_lists(jax.random.fold_in(arg_keys[4], 71), 0)
    pair_count = draw_pair_count(jax.random.fold_in(arg_keys[4], 71), 0)
    return {"left_blocks": left_blocks, "right_blocks": right_blocks, "pair_lists": pair_lists, "pair_count": pair_count}


def reference(left_blocks, right_blocks, pair_lists, pair_count):
    per_col = N_ROW // N_COL
    left_all = left_blocks.reshape(N_ROW, NA, N_COL, BS, BS).transpose(0, 2, 1, 3, 4)
    grid_rows = jnp.arange(N_ROW, dtype=jnp.int32)[:, None]
    grid_inner = jnp.arange(N_COL, dtype=jnp.int32)[None, :]
    left_tiles = left_all[grid_rows, (grid_inner - grid_rows) % N_COL]
    right_all = right_blocks.reshape(N_COL, NB, N_ROW, BS, BS).transpose(0, 2, 1, 3, 4)
    block_cols = jnp.arange(N_ROW, dtype=jnp.int32)[None, :]
    inner_rows = jnp.arange(N_COL, dtype=jnp.int32)[:, None]
    owner_col = block_cols // per_col
    seat_index = (block_cols % per_col) * N_COL + inner_rows
    owner_row = (seat_index - owner_col) % N_ROW
    right_tiles = right_all[owner_col, owner_row]
    pairs_all = pair_lists.reshape(N_ROW, N_ROW, N_COL, NT, 3)
    count_all = pair_count.reshape(N_ROW, N_ROW, N_COL)
    inner_index = jnp.arange(N_COL, dtype=jnp.int32)[:, None]
    slot_index = jnp.arange(NT, dtype=jnp.int32)[None, :]
    target_index = jnp.arange(NC, dtype=jnp.int32)

    def one_row(row_index):
        left_row = left_tiles[row_index]

        def one_block(col_index):
            right_col = right_tiles[:, col_index]
            pairs_now = pairs_all[row_index, col_index]
            valid = slot_index < count_all[row_index, col_index][:, None]
            left_pick = left_row[inner_index, pairs_now[..., 0]].astype(jnp.float32)
            right_pick = right_col[inner_index, pairs_now[..., 1]].astype(jnp.float32)
            products = jnp.einsum("ktrx,ktxc->ktrc", left_pick, right_pick)
            weight = ((pairs_now[..., 2][..., None] == target_index) & valid[..., None]).astype(jnp.float32)
            return jnp.einsum("ktrc,ktn->nrc", products, weight, precision=lax.Precision.HIGHEST)

        return lax.map(one_block, jnp.arange(N_ROW, dtype=jnp.int32))

    result = lax.map(one_row, jnp.arange(N_ROW, dtype=jnp.int32))
    return result.reshape(N_ROW * N_ROW * NC, BS, BS).astype(jnp.bfloat16)
```

```python
import jax
import jax.numpy as jnp
from jax import lax
from jax.experimental import pallas as pl
from jax.experimental.pallas import tpu as pltpu
from jax.sharding import Mesh
from jax.sharding import PartitionSpec as P

NX, NZL, NZH, NY, NCORE = 8, 4, 2, 8, 2
NK = 32
NA, NB, NC, NT = 4, 2, 2, 8
BS = 128
GROUP = 8
ZERO = NK * NB


def rot(size, shift):
    return [(s, (s + shift) % size) for s in range(size)]


def slot_lists(pair_lists, pair_count, row, col, zh, y, c):
    pairs = pair_lists.reshape(NK * NT, 3)
    flat = jnp.arange(NK * NT, dtype=jnp.int32)
    k = flat // NT
    live = flat % NT < jnp.repeat(pair_count.reshape(NK), NT)
    source = (k - row) % NK
    from_zh, from_y, from_c = source // (NY * NCORE), source // NCORE % NY, source % NCORE
    place = jnp.where(from_c == c, 0, NY) + (from_y - y) % NY
    place = place * 2 + jnp.where(from_zh == zh, 0, 1)
    left = place * NA + pairs[:, 0]
    right = (k - col) % NK * NB + pairs[:, 1]
    code = left * 128 + right
    target = jnp.arange(NC, dtype=jnp.int32)[:, None]
    mine = live[None] & (pairs[:, 2][None] == target)
    seat = jnp.sum(mine[:, None, :] & (flat[None, None, :] < flat[None, :, None]), axis=-1)
    hit = mine[:, :, None] & (seat[:, :, None] == flat[None, None, :])
    listed = jnp.sum(jnp.where(hit, code[None, :, None] - ZERO, 0), axis=1) + ZERO
    return listed.astype(jnp.int32), jnp.sum(mine, axis=1).astype(jnp.int32)


def product_kernel(plan, codes, counts, *refs):
    pieces, (out, left, right, sems) = refs[: len(refs) - 4], refs[len(refs) - 4 :]
    copies = []
    for piece, (which, start, size, at) in plan:
        target = right if which else left
        copies.append(
            pltpu.make_async_copy(
                pieces[piece].at[pl.ds(start, size)],
                target.at[pl.ds(at, size)],
                sems.at[len(copies)],
            )
        )
    for copy in copies:
        copy.start()
    right[ZERO] = jnp.zeros((BS, BS), jnp.bfloat16)
    for copy in copies:
        copy.wait()

    def part(n, step):
        first, second = [], []
        for g in range(GROUP):
            code = codes[n, step * GROUP + g]
            first.append(left[code // 128])
            second.append(right[code % 128])
        return jnp.dot(
            jnp.concatenate(first, axis=1),
            jnp.concatenate(second, axis=0),
            preferred_element_type=jnp.float32,
        )

    steps = (jnp.maximum(counts[0], counts[1]) + GROUP - 1) // GROUP
    zero = jnp.zeros((BS, BS), jnp.float32)

    def step(turn, total):
        return total[0] + part(0, turn), total[1] + part(1, turn)

    total = lax.fori_loop(0, steps, step, (zero, zero))
    out[0] = total[0].astype(jnp.bfloat16)
    out[1] = total[1].astype(jnp.bfloat16)


def per_device(left_blocks, right_blocks, pair_lists, pair_count):
    zh, y, c = lax.axis_index("zh"), lax.axis_index("y"), lax.axis_index("c")
    row = lax.axis_index("x") * NZL + lax.axis_index("zl")
    col = (zh * NY + y) * NCORE + c

    other = lax.ppermute(left_blocks, "zh", rot(NZH, 1))
    spread = jnp.broadcast_to(right_blocks[None], (NZL,) + right_blocks.shape)
    right_z = lax.all_to_all(spread.reshape(NZL * NB, BS, BS), "zl", 0, 0, tiled=True)
    right_all = lax.all_gather(right_z, "x", axis=0, tiled=True)

    base = jnp.concatenate([left_blocks, other], axis=0)
    up, down = [base], [base]
    for _ in range(3):
        up.append(lax.ppermute(up[-1], "y", rot(NY, 1)))
        down.append(lax.ppermute(down[-1], "y", rot(NY, -1)))
    up.append(lax.ppermute(up[3][:NA], "y", rot(NY, 1)))
    down.append(lax.ppermute(down[3][NA:], "y", rot(NY, -1)))

    near = jnp.concatenate([base, up[1], down[1], up[2], down[2]], axis=0)
    far = jnp.concatenate([up[3], down[3], up[4], down[4]], axis=0)
    near_swap = lax.ppermute(near, "c", rot(NCORE, 1))
    far_swap = lax.ppermute(far, "c", rot(NCORE, 1))

    codes, counts = slot_lists(pair_lists, pair_count, row, col, zh, y, c)

    tile = 2 * NA
    plan = []
    for half, (near_piece, far_piece) in enumerate(((0, 1), (2, 3))):
        for at, distance in enumerate((0, -1, 1, -2, 2)):
            plan.append((near_piece, (0, at * tile, tile, (half * NY + distance % NY) * tile)))
        for at, distance in enumerate((-3, 3, 4)):
            plan.append((far_piece, (0, at * tile, tile, (half * NY + distance % NY) * tile)))
    plan.append((4, (1, 0, ZERO, 0)))

    def kernel(*refs):
        product_kernel(plan, *refs)

    return pl.pallas_call(
        kernel,
        out_shape=jax.ShapeDtypeStruct((NC, BS, BS), jnp.bfloat16),
        in_specs=[pl.BlockSpec(memory_space=pltpu.SMEM)] * 2
        + [pl.BlockSpec(memory_space=pl.ANY)] * 5,
        out_specs=pl.BlockSpec(memory_space=pltpu.VMEM),
        scratch_shapes=[
            pltpu.VMEM((2 * NY * tile, BS, BS), jnp.bfloat16),
            pltpu.VMEM((ZERO + 1, BS, BS), jnp.bfloat16),
            pltpu.SemaphoreType.DMA((len(plan),)),
        ],
        compiler_params=pltpu.CompilerParams(vmem_limit_bytes=16 * 1024 * 1024),
        cost_estimate=pl.CostEstimate(
            flops=2 * 128 * BS**3, bytes_accessed=6 * 1024 * 1024, transcendentals=0
        ),
        name="block_products",
    )(codes, counts, near, far, near_swap, far_swap, right_all)


def solution(mesh):
    parts = Mesh(mesh.devices.reshape(NX, NZL, NZH, NY, NCORE), ("x", "zl", "zh", "y", "c"))
    row, col = ("x", "zl"), ("zh", "y", "c")
    return jax.shard_map(
        per_device,
        mesh=parts,
        in_specs=(P(row, col, None), P(col, row, None), P(row + col, None, None), P(row + col, None)),
        out_specs=P(row + col, None, None),
        check_vma=False,
    )
```

```python
import jax
import jax.numpy as jnp
from jax import lax
from jax.experimental import pallas as pl
from jax.experimental.pallas import tpu as pltpu
from jax.sharding import Mesh
from jax.sharding import PartitionSpec as P

NX, NZL, NZH, NY, NCORE = 8, 4, 2, 8, 2
NK = 32
NA, NB, NC, NT = 4, 2, 2, 8
BS = 128
GROUP = 8
TILE = 16
ZERO = 2 * NY * TILE


def rot(size, shift):
    return [(s, (s + shift) % size) for s in range(size)]


def slot_lists(pair_lists, pair_count, x, zl, zh, y, c):
    pairs = pair_lists.reshape(NK * NT, 3)
    flat = jnp.arange(NK * NT, dtype=jnp.int32)
    k = flat // NT
    live = flat % NT < jnp.repeat(pair_count.reshape(NK), NT)
    row, col = x * NZL + zl, (zh * NY + y) * NCORE + c
    source = (k - row) % NK
    from_zh, from_y, from_c = source // (NY * NCORE), source // NCORE % NY, source % NCORE
    near = from_zh == zh
    part = jnp.where(from_c == 0, jnp.where(near, 0, 1), jnp.where(near, 3, 2))
    left = (jnp.where(c == 1, 0, NY) + (from_y - y) % NY) * TILE + part * NA + pairs[:, 0]
    holder = (k - col) % NK
    part = (zl - holder % NZL) % NZL
    right = (jnp.where(c == 0, 0, NY) + (holder // NZL - x) % NX) * TILE
    right = right + (part * NCORE + c) * NB + pairs[:, 1]
    code = left * 512 + right
    target = jnp.arange(NC, dtype=jnp.int32)[:, None]
    mine = live[None] & (pairs[:, 2][None] == target)
    seat = jnp.sum(mine[:, None, :] & (flat[None, None, :] < flat[None, :, None]), axis=-1)
    hit = mine[:, :, None] & (seat[:, :, None] == flat[None, None, :])
    listed = jnp.sum(jnp.where(hit, code[None, :, None] - ZERO, 0), axis=1) + ZERO
    return listed.astype(jnp.int32), jnp.sum(mine, axis=1).astype(jnp.int32)


def product_kernel(plan, codes, counts, *refs):
    pieces, (out, held, sems) = refs[:-3], refs[-3:]
    copies = []
    for piece, (size, at) in zip(pieces, plan, strict=True):
        copies.append(
            pltpu.make_async_copy(piece, held.at[pl.ds(at, size)], sems.at[len(copies)])
        )
    for copy in copies:
        copy.start()
    held[ZERO] = jnp.zeros((BS, BS), jnp.bfloat16)
    for copy in copies:
        copy.wait()

    def part(n, step):
        first, second = [], []
        for g in range(GROUP):
            code = codes[n, step * GROUP + g]
            first.append(held[code // 512])
            second.append(held[code % 512])
        return jnp.dot(
            jnp.concatenate(first, axis=1),
            jnp.concatenate(second, axis=0),
            preferred_element_type=jnp.float32,
        )

    steps = (jnp.maximum(counts[0], counts[1]) + GROUP - 1) // GROUP
    zero = jnp.zeros((BS, BS), jnp.float32)

    def step(turn, total):
        return total[0] + part(0, turn), total[1] + part(1, turn)

    total = lax.fori_loop(0, steps, step, (zero, zero))
    out[0] = total[0].astype(jnp.bfloat16)
    out[1] = total[1].astype(jnp.bfloat16)


def along_plane(value, shift):
    pairs = []
    for x in range(NX):
        for y in range(NY):
            place = (x * NY + y) * NCORE
            pairs.append((place, ((x + shift) % NX * NY + y) * NCORE))
            pairs.append((place + 1, (x * NY + (y + shift) % NY) * NCORE + 1))
    return lax.ppermute(value, ("x", "y", "c"), pairs)


def along_z(value, shift, swap):
    pairs = []
    for zl in range(NZL):
        for zh in range(NZH):
            place = (zl * NZH + zh) * NCORE
            pairs.append((place, ((zl + shift) % NZL * NZH + zh) * NCORE))
            pairs.append((place + 1, (zl * NZH + (zh + swap) % NZH) * NCORE + 1))
    return lax.ppermute(value, ("zl", "zh", "c"), pairs)


def to_partner(value):
    return lax.ppermute(value, "c", rot(NCORE, 1))


def per_device(left_blocks, right_blocks, pair_lists, pair_count):
    x, zl, zh, y, c = (lax.axis_index(name) for name in ("x", "zl", "zh", "y", "c"))

    got = to_partner(jnp.where(c == 0, left_blocks, jnp.concatenate([right_blocks] * 2)))
    rights = jnp.concatenate([right_blocks, got[:NB]])
    first, second = jnp.where(c == 0, rights, got), jnp.where(c == 0, rights, left_blocks)
    own = jnp.concatenate(
        [first, along_z(first, 1, 1), along_z(second, 2, 1), along_z(second, 3, 0)]
    )
    up, down = [own], [own]
    for _ in range(3):
        up.append(along_plane(up[-1], 1))
        down.append(along_plane(down[-1], -1))
    up.append(along_plane(up[2][: TILE // 2], 2))
    down.append(along_plane(down[2][TILE // 2 :], -2))

    pieces, plan = [own], [(TILE, 0)]
    for distance in range(1, 4):
        pieces += [up[distance], down[distance]]
        plan += [(TILE, (NY - distance) * TILE), (TILE, distance * TILE)]
    pieces += [up[4], down[4]]
    plan += [(TILE // 2, 4 * TILE), (TILE // 2, 4 * TILE + TILE // 2)]
    pieces += [to_partner(piece) for piece in pieces]
    plan += [(size, NY * TILE + at) for size, at in plan]

    codes, counts = slot_lists(pair_lists, pair_count, x, zl, zh, y, c)

    def kernel(*refs):
        product_kernel(plan, *refs)

    return pl.pallas_call(
        kernel,
        out_shape=jax.ShapeDtypeStruct((NC, BS, BS), jnp.bfloat16),
        in_specs=[pl.BlockSpec(memory_space=pltpu.SMEM)] * 2
        + [pl.BlockSpec(memory_space=pl.ANY)] * len(pieces),
        out_specs=pl.BlockSpec(memory_space=pltpu.VMEM),
        scratch_shapes=[
            pltpu.VMEM((ZERO + 1, BS, BS), jnp.bfloat16),
            pltpu.SemaphoreType.DMA((len(plan),)),
        ],
        compiler_params=pltpu.CompilerParams(vmem_limit_bytes=16 * 1024 * 1024),
        cost_estimate=pl.CostEstimate(
            flops=2 * 128 * BS**3, bytes_accessed=6 * 1024 * 1024, transcendentals=0
        ),
        name="block_products",
    )(codes, counts, *pieces)


def solution(mesh):
    parts = Mesh(mesh.devices.reshape(NX, NZL, NZH, NY, NCORE), ("x", "zl", "zh", "y", "c"))
    row, col = ("x", "zl"), ("zh", "y", "c")
    return jax.shard_map(
        per_device,
        mesh=parts,
        in_specs=(P(row, col, None), P(col, row, None), P(row + col, None, None), P(row + col, None)),
        out_specs=P(row + col, None, None),
        check_vma=False,
    )
```

```python
import jax
import jax.numpy as jnp
from jax import lax
from jax.experimental import pallas as pl
from jax.experimental.pallas import tpu as pltpu
from jax.sharding import Mesh
from jax.sharding import PartitionSpec as P

NX, NZL, NZH, NY, NCORE = 8, 4, 2, 8, 2
NK = 32
NA, NB, NC, NT = 4, 2, 2, 8
BS = 128
GROUP = 8
TILE = 16
ZERO = 2 * NY * TILE
SEATS = (0, 6, 3, 5, 1, 7, 2, 4)


def rot(size, shift):
    return [(s, (s + shift) % size) for s in range(size)]


def seat_of(distance):
    hit = distance[:, None] % NY == jnp.arange(NY, dtype=jnp.int32)
    return jnp.sum(jnp.where(hit, jnp.array(SEATS, jnp.int32), 0), axis=1)


def slot_lists(pair_lists, pair_count, x, zl, zh, y, c):
    pairs = pair_lists.reshape(NK * NT, 3)
    flat = jnp.arange(NK * NT, dtype=jnp.int32)
    k = flat // NT
    live = flat % NT < jnp.repeat(pair_count.reshape(NK), NT)
    row, col = x * NZL + zl, (zh * NY + y) * NCORE + c
    source = (k - row) % NK
    from_zh, from_y, from_c = source // (NY * NCORE), source // NCORE % NY, source % NCORE
    near = from_zh == zh
    part = jnp.where(from_c == 0, jnp.where(near, 0, 1), jnp.where(near, 3, 2))
    left = (jnp.where(c == 1, 0, NY) + seat_of(from_y - y)) * TILE + part * NA + pairs[:, 0]
    holder = (k - col) % NK
    part = (zl - holder % NZL) % NZL
    right = (jnp.where(c == 0, 0, NY) + seat_of(holder // NZL - x)) * TILE
    right = right + (part * NCORE + c) * NB + pairs[:, 1]
    code = left * 512 + right
    target = jnp.arange(NC, dtype=jnp.int32)[:, None]
    mine = live[None] & (pairs[:, 2][None] == target)
    seat = jnp.sum(mine[:, None, :] & (flat[None, None, :] < flat[None, :, None]), axis=-1)
    hit = mine[:, :, None] & (seat[:, :, None] == flat[None, None, :])
    listed = jnp.sum(jnp.where(hit, code[None, :, None] - ZERO, 0), axis=1) + ZERO
    return listed.astype(jnp.int32), jnp.sum(mine, axis=1).astype(jnp.int32)


def product_kernel(plan, codes, counts, *refs):
    pieces, (out, held, sems) = refs[:-3], refs[-3:]
    copies = []
    for piece, (size, at) in zip(pieces, plan, strict=True):
        copies.append(
            pltpu.make_async_copy(piece, held.at[pl.ds(at, size)], sems.at[len(copies)])
        )
    for copy in copies:
        copy.start()
    held[ZERO] = jnp.zeros((BS, BS), jnp.bfloat16)
    for copy in copies:
        copy.wait()

    def part(n, step):
        first, second = [], []
        for g in range(GROUP):
            code = codes[n, step * GROUP + g]
            first.append(held[code // 512])
            second.append(held[code % 512])
        return jnp.dot(
            jnp.concatenate(first, axis=1),
            jnp.concatenate(second, axis=0),
            preferred_element_type=jnp.float32,
        )

    steps = (jnp.maximum(counts[0], counts[1]) + GROUP - 1) // GROUP
    zero = jnp.zeros((BS, BS), jnp.float32)

    def step(turn, total):
        return total[0] + part(0, turn), total[1] + part(1, turn)

    total = lax.fori_loop(0, steps, step, (zero, zero))
    out[0] = total[0].astype(jnp.bfloat16)
    out[1] = total[1].astype(jnp.bfloat16)


def along_plane(value, shift):
    pairs = []
    for x in range(NX):
        for y in range(NY):
            place = (x * NY + y) * NCORE
            pairs.append((place, ((x + shift) % NX * NY + y) * NCORE))
            pairs.append((place + 1, (x * NY + (y + shift) % NY) * NCORE + 1))
    return lax.ppermute(value, ("x", "y", "c"), pairs)


def along_z(value, shift, swap):
    pairs = []
    for zl in range(NZL):
        for zh in range(NZH):
            place = (zl * NZH + zh) * NCORE
            pairs.append((place, ((zl + shift) % NZL * NZH + zh) * NCORE))
            pairs.append((place + 1, (zl * NZH + (zh + swap) % NZH) * NCORE + 1))
    return lax.ppermute(value, ("zl", "zh", "c"), pairs)


def to_partner(value):
    return lax.ppermute(value, "c", rot(NCORE, 1))


def per_device(left_blocks, right_blocks, pair_lists, pair_count):
    x, zl, zh, y, c = (lax.axis_index(name) for name in ("x", "zl", "zh", "y", "c"))

    got = to_partner(jnp.where(c == 0, left_blocks, jnp.concatenate([right_blocks] * 2)))
    rights = jnp.concatenate([right_blocks, got[:NB]])
    first, second = jnp.where(c == 0, rights, got), jnp.where(c == 0, rights, left_blocks)
    own = jnp.concatenate(
        [first, along_z(first, 1, 1), along_z(second, 2, 1), along_z(second, 3, 0)]
    )
    pair = jnp.concatenate([own, along_plane(own, NY // 2)])
    pieces = [pair, along_plane(own, 2), along_plane(own, -2)]
    pieces += [along_plane(pair, 1), along_plane(pair, -1)]
    pieces += [to_partner(piece) for piece in pieces]
    plan, at = [], 0
    for piece in pieces:
        plan.append((piece.shape[0], at))
        at += piece.shape[0]

    codes, counts = slot_lists(pair_lists, pair_count, x, zl, zh, y, c)

    def kernel(*refs):
        product_kernel(plan, *refs)

    return pl.pallas_call(
        kernel,
        out_shape=jax.ShapeDtypeStruct((NC, BS, BS), jnp.bfloat16),
        in_specs=[pl.BlockSpec(memory_space=pltpu.SMEM)] * 2
        + [pl.BlockSpec(memory_space=pl.ANY)] * len(pieces),
        out_specs=pl.BlockSpec(memory_space=pltpu.VMEM),
        scratch_shapes=[
            pltpu.VMEM((ZERO + 1, BS, BS), jnp.bfloat16),
            pltpu.SemaphoreType.DMA((len(plan),)),
        ],
        compiler_params=pltpu.CompilerParams(vmem_limit_bytes=16 * 1024 * 1024),
        cost_estimate=pl.CostEstimate(
            flops=2 * 128 * BS**3, bytes_accessed=6 * 1024 * 1024, transcendentals=0
        ),
        name="block_products",
    )(codes, counts, *pieces)


def solution(mesh):
    parts = Mesh(mesh.devices.reshape(NX, NZL, NZH, NY, NCORE), ("x", "zl", "zh", "y", "c"))
    row, col = ("x", "zl"), ("zh", "y", "c")
    return jax.shard_map(
        per_device,
        mesh=parts,
        in_specs=(P(row, col, None), P(col, row, None), P(row + col, None, None), P(row + col, None)),
        out_specs=P(row + col, None, None),
        check_vma=False,
    )
```

```python
import jax
import jax.numpy as jnp
from jax import lax
from jax.experimental import pallas as pl
from jax.experimental.pallas import tpu as pltpu
from jax.sharding import Mesh
from jax.sharding import PartitionSpec as P

NX, NZL, NZH, NY, NCORE = 8, 4, 2, 8, 2
NK = 32
NA, NB, NC, NT = 4, 2, 2, 8
BS = 128
GROUP = 16
TILE = 16
ZERO = 2 * NY * TILE
SEATS = (1, 5, 2, 6, 7, 3, 0, 4)


def rot(size, shift):
    return [(s, (s + shift) % size) for s in range(size)]


def seat_of(distance):
    hit = distance[:, None] % NY == jnp.arange(NY, dtype=jnp.int32)
    return jnp.sum(jnp.where(hit, jnp.array(SEATS, jnp.int32), 0), axis=1)


def slot_lists(pair_lists, pair_count, x, zl, zh, y, c):
    pairs = pair_lists.reshape(NK * NT, 3)
    flat = jnp.arange(NK * NT, dtype=jnp.int32)
    k = flat // NT
    live = flat % NT < jnp.repeat(pair_count.reshape(NK), NT)
    row, col = x * NZL + zl, (zh * NY + y) * NCORE + c
    source = (k - row) % NK
    from_zh, from_y, from_c = source // (NY * NCORE), source // NCORE % NY, source % NCORE
    near = from_zh == zh
    part = jnp.where(from_c == 0, jnp.where(near, 0, 1), jnp.where(near, 3, 2))
    left = (jnp.where(c == 1, 0, NY) + seat_of(from_y - y)) * TILE + part * NA + pairs[:, 0]
    holder = (k - col) % NK
    part = (zl - holder % NZL) % NZL
    right = (jnp.where(c == 0, 0, NY) + seat_of(holder // NZL - x)) * TILE
    right = right + (part * NCORE + c) * NB + pairs[:, 1]
    code = left * 512 + right
    target = jnp.arange(NC, dtype=jnp.int32)[:, None]
    mine = live[None] & (pairs[:, 2][None] == target)
    seat = jnp.sum(mine[:, None, :] & (flat[None, None, :] < flat[None, :, None]), axis=-1)
    hit = mine[:, :, None] & (seat[:, :, None] == flat[None, None, :])
    listed = jnp.sum(jnp.where(hit, code[None, :, None] - ZERO, 0), axis=1) + ZERO
    return listed.astype(jnp.int32), jnp.sum(mine, axis=1).astype(jnp.int32)


def product_kernel(plan, codes, counts, *refs):
    pieces, (out, held, sems) = refs[:-3], refs[-3:]
    copies = []
    for piece, (size, at) in zip(pieces, plan, strict=True):
        copies.append(
            pltpu.make_async_copy(piece, held.at[pl.ds(at, size)], sems.at[len(copies)])
        )
    for copy in copies:
        copy.start()
    held[ZERO] = jnp.zeros((BS, BS), jnp.bfloat16)
    for copy in copies:
        copy.wait()

    def part(n, step):
        first, second = [], []
        for g in range(GROUP):
            code = codes[n, step * GROUP + g]
            first.append(held[code // 512])
            second.append(held[code % 512])
        return jnp.dot(
            jnp.concatenate(first, axis=1),
            jnp.concatenate(second, axis=0),
            preferred_element_type=jnp.float32,
        )

    steps = (jnp.maximum(counts[0], counts[1]) + GROUP - 1) // GROUP
    zero = jnp.zeros((BS, BS), jnp.float32)

    def step(turn, total):
        return total[0] + part(0, turn), total[1] + part(1, turn)

    total = lax.fori_loop(0, steps, step, (zero, zero))
    out[0] = total[0].astype(jnp.bfloat16)
    out[1] = total[1].astype(jnp.bfloat16)


def along_plane(value, shift):
    pairs = []
    for x in range(NX):
        for y in range(NY):
            place = (x * NY + y) * NCORE
            pairs.append((place, ((x + shift) % NX * NY + y) * NCORE))
            pairs.append((place + 1, (x * NY + (y + shift) % NY) * NCORE + 1))
    return lax.ppermute(value, ("x", "y", "c"), pairs)


def along_z(value, shift, swap):
    pairs = []
    for zl in range(NZL):
        for zh in range(NZH):
            place = (zl * NZH + zh) * NCORE
            pairs.append((place, ((zl + shift) % NZL * NZH + zh) * NCORE))
            pairs.append((place + 1, (zl * NZH + (zh + swap) % NZH) * NCORE + 1))
    return lax.ppermute(value, ("zl", "zh", "c"), pairs)


def to_partner(value):
    return lax.ppermute(value, "c", rot(NCORE, 1))


def per_device(left_blocks, right_blocks, pair_lists, pair_count):
    x, zl, zh, y, c = (lax.axis_index(name) for name in ("x", "zl", "zh", "y", "c"))

    got = to_partner(jnp.where(c == 0, left_blocks, jnp.concatenate([right_blocks] * 2)))
    rights = jnp.concatenate([right_blocks, got[:NB]])
    first, second = jnp.where(c == 0, rights, got), jnp.where(c == 0, rights, left_blocks)
    own = jnp.concatenate(
        [first, along_z(first, 1, 1), along_z(second, 2, 1), along_z(second, 3, 0)]
    )
    half = TILE // 2
    behind, ahead = along_plane(own, 2), along_plane(own, -2)
    near = jnp.concatenate([behind, own, ahead])
    pieces = [near, along_plane(near[: 2 * TILE], 1), along_plane(near[TILE:], -1)]
    far = [along_plane(behind[:half], 2), along_plane(ahead[half:], -2)]
    pieces.append(jnp.concatenate(far))
    pieces += [to_partner(piece) for piece in pieces]
    plan, at = [], 0
    for piece in pieces:
        plan.append((piece.shape[0], at))
        at += piece.shape[0]

    codes, counts = slot_lists(pair_lists, pair_count, x, zl, zh, y, c)

    def kernel(*refs):
        product_kernel(plan, *refs)

    return pl.pallas_call(
        kernel,
        out_shape=jax.ShapeDtypeStruct((NC, BS, BS), jnp.bfloat16),
        in_specs=[pl.BlockSpec(memory_space=pltpu.SMEM)] * 2
        + [pl.BlockSpec(memory_space=pl.ANY)] * len(pieces),
        out_specs=pl.BlockSpec(memory_space=pltpu.VMEM),
        scratch_shapes=[
            pltpu.VMEM((ZERO + 1, BS, BS), jnp.bfloat16),
            pltpu.SemaphoreType.DMA((len(plan),)),
        ],
        compiler_params=pltpu.CompilerParams(vmem_limit_bytes=16 * 1024 * 1024),
        cost_estimate=pl.CostEstimate(
            flops=2 * 128 * BS**3, bytes_accessed=6 * 1024 * 1024, transcendentals=0
        ),
        name="block_products",
    )(codes, counts, *pieces)


def solution(mesh):
    parts = Mesh(mesh.devices.reshape(NX, NZL, NZH, NY, NCORE), ("x", "zl", "zh", "y", "c"))
    row, col = ("x", "zl"), ("zh", "y", "c")
    return jax.shard_map(
        per_device,
        mesh=parts,
        in_specs=(P(row, col, None), P(col, row, None), P(row + col, None, None), P(row + col, None)),
        out_specs=P(row + col, None, None),
        check_vma=False,
    )
```

```python
import jax
import jax.numpy as jnp
from jax import lax
from jax.experimental import pallas as pl
from jax.experimental.pallas import tpu as pltpu
from jax.sharding import Mesh
from jax.sharding import PartitionSpec as P

NX, NZL, NZH, NY, NCORE = 8, 4, 2, 8, 2
NK = 32
NA, NB, NC, NT = 4, 2, 2, 8
BS = 128
GROUP = 16
TILE = 8
ZERO = 3 * NY * TILE
SEATS = (1, 5, 2, 6, 7, 3, 0, 4)


def rot(size, shift):
    return [(s, (s + shift) % size) for s in range(size)]


def seat_of(distance):
    hit = distance[:, None] % NY == jnp.arange(NY, dtype=jnp.int32)
    return jnp.sum(jnp.where(hit, jnp.array(SEATS, jnp.int32), 0), axis=1)


def slot_lists(pair_lists, pair_count, x, zl, zh, y, c):
    pairs = pair_lists.reshape(NK * NT, 3)
    flat = jnp.arange(NK * NT, dtype=jnp.int32)
    k = flat // NT
    live = flat % NT < jnp.repeat(pair_count.reshape(NK), NT)
    row, col = x * NZL + zl, (zh * NY + y) * NCORE + c
    source = (k - row) % NK
    from_zh, from_y, from_c = source // (NY * NCORE), source // NCORE % NY, source % NCORE
    left = (jnp.where(from_c == c, 0, NY) + from_y) * TILE + pairs[:, 0]
    left = left + jnp.where(from_zh == zh, 0, NA)
    holder = (k - col) % NK
    right = (2 * NY + seat_of(holder // NZL - x)) * TILE
    right = right + (zl - holder % NZL) % NZL * NB + pairs[:, 1]
    code = left * 256 + right
    target = jnp.arange(NC, dtype=jnp.int32)[:, None]
    mine = live[None] & (pairs[:, 2][None] == target)
    seat = jnp.sum(mine[:, None, :] & (flat[None, None, :] < flat[None, :, None]), axis=-1)
    hit = mine[:, :, None] & (seat[:, :, None] == flat[None, None, :])
    listed = jnp.sum(jnp.where(hit, code[None, :, None] - ZERO, 0), axis=1) + ZERO
    return listed.astype(jnp.int32), jnp.sum(mine, axis=1).astype(jnp.int32)


def product_kernel(plan, codes, counts, *refs):
    pieces, (out, held, sems) = refs[:-3], refs[-3:]
    copies = []
    for piece, (size, at) in zip(pieces, plan, strict=True):
        copies.append(
            pltpu.make_async_copy(piece, held.at[pl.ds(at, size)], sems.at[len(copies)])
        )
    for copy in copies:
        copy.start()
    held[ZERO] = jnp.zeros((BS, BS), jnp.bfloat16)
    for copy in copies:
        copy.wait()

    def part(n, step):
        first, second = [], []
        for g in range(GROUP):
            code = codes[n, step * GROUP + g]
            first.append(held[code // 256])
            second.append(held[code % 256])
        return jnp.dot(
            jnp.concatenate(first, axis=1),
            jnp.concatenate(second, axis=0),
            preferred_element_type=jnp.float32,
        )

    steps = (jnp.maximum(counts[0], counts[1]) + GROUP - 1) // GROUP
    zero = jnp.zeros((BS, BS), jnp.float32)

    def step(turn, total):
        return total[0] + part(0, turn), total[1] + part(1, turn)

    total = lax.fori_loop(0, steps, step, (zero, zero))
    out[0] = total[0].astype(jnp.bfloat16)
    out[1] = total[1].astype(jnp.bfloat16)


def per_device(left_blocks, right_blocks, pair_lists, pair_count):
    x, zl, zh, y, c = (lax.axis_index(name) for name in ("x", "zl", "zh", "y", "c"))

    own = [right_blocks]
    own += [lax.ppermute(right_blocks, "zl", rot(NZL, shift)) for shift in range(1, NZL)]
    own = jnp.concatenate(own)
    lefts = jnp.concatenate([left_blocks, lax.ppermute(left_blocks, "zh", rot(NZH, 1))])
    lefts, own = lax.optimization_barrier((lefts, own))
    spread = jnp.broadcast_to(lefts[None], (NY,) + lefts.shape).reshape(NY * TILE, BS, BS)
    lefts = lax.all_to_all(spread, "y", 0, 0, tiled=True)

    half = TILE // 2
    behind = lax.ppermute(own, "x", rot(NX, 2))
    ahead = lax.ppermute(own, "x", rot(NX, -2))
    behind, ahead = lax.optimization_barrier((behind, ahead))
    near = jnp.concatenate([behind, own, ahead])
    rights = [near]
    rights.append(lax.ppermute(near[: 2 * TILE], "x", rot(NX, 1)))
    rights.append(lax.ppermute(near[TILE:], "x", rot(NX, -1)))
    rights.append(lax.ppermute(behind[:half], "x", rot(NX, 2)))
    rights.append(lax.ppermute(ahead[half:], "x", rot(NX, -2)))

    lefts, *rights = lax.optimization_barrier((lefts, *rights))
    pieces = [lefts, lax.ppermute(lefts, "c", rot(NCORE, 1))] + rights
    plan, at = [], 0
    for piece in pieces:
        plan.append((piece.shape[0], at))
        at += piece.shape[0]

    codes, counts = slot_lists(pair_lists, pair_count, x, zl, zh, y, c)

    def kernel(*refs):
        product_kernel(plan, *refs)

    return pl.pallas_call(
        kernel,
        out_shape=jax.ShapeDtypeStruct((NC, BS, BS), jnp.bfloat16),
        in_specs=[pl.BlockSpec(memory_space=pltpu.SMEM)] * 2
        + [pl.BlockSpec(memory_space=pl.ANY)] * len(pieces),
        out_specs=pl.BlockSpec(memory_space=pltpu.VMEM),
        scratch_shapes=[
            pltpu.VMEM((ZERO + 1, BS, BS), jnp.bfloat16),
            pltpu.SemaphoreType.DMA((len(plan),)),
        ],
        compiler_params=pltpu.CompilerParams(vmem_limit_bytes=16 * 1024 * 1024),
        cost_estimate=pl.CostEstimate(
            flops=2 * 128 * BS**3, bytes_accessed=6 * 1024 * 1024, transcendentals=0
        ),
        name="block_products",
    )(codes, counts, *pieces)


def solution(mesh):
    parts = Mesh(mesh.devices.reshape(NX, NZL, NZH, NY, NCORE), ("x", "zl", "zh", "y", "c"))
    row, col = ("x", "zl"), ("zh", "y", "c")
    return jax.shard_map(
        per_device,
        mesh=parts,
        in_specs=(P(row, col, None), P(col, row, None), P(row + col, None, None), P(row + col, None)),
        out_specs=P(row + col, None, None),
        check_vma=False,
    )
```

```python
import jax
import jax.numpy as jnp
from jax import lax
from jax.experimental import pallas as pl
from jax.experimental.pallas import tpu as pltpu
from jax.sharding import Mesh
from jax.sharding import PartitionSpec as P

NX, NZL, NZH, NY, NCORE = 8, 4, 2, 8, 2
NK = 32
NA, NB, NC, NT = 4, 2, 2, 8
BS = 128
GROUP = 16
TILE = 16
ZERO = 2 * NY * TILE
SEATS = (0, 2, 4, 6, 7, 5, 3, 1)


def rot(size, shift):
    return [(s, (s + shift) % size) for s in range(size)]


def seat_of(distance):
    hit = distance[:, None] % NY == jnp.arange(NY, dtype=jnp.int32)
    return jnp.sum(jnp.where(hit, jnp.array(SEATS, jnp.int32), 0), axis=1)


def slot_lists(pair_lists, pair_count, x, zl, zh, y, c):
    pairs = pair_lists.reshape(NK * NT, 3)
    flat = jnp.arange(NK * NT, dtype=jnp.int32)
    k = flat // NT
    live = flat % NT < jnp.repeat(pair_count.reshape(NK), NT)
    row, col = x * NZL + zl, (zh * NY + y) * NCORE + c
    source = (k - row) % NK
    from_zh, from_y, from_c = source // (NY * NCORE), source // NCORE % NY, source % NCORE
    near = from_zh == zh
    part = jnp.where(from_c == 0, jnp.where(near, 0, 1), jnp.where(near, 3, 2))
    left = (jnp.where(c == 1, 0, NY) + seat_of(from_y - y)) * TILE + part * NA + pairs[:, 0]
    holder = (k - col) % NK
    part = (zl - holder % NZL) % NZL
    right = (jnp.where(c == 0, 0, NY) + seat_of(holder // NZL - x)) * TILE
    right = right + (part * NCORE + c) * NB + pairs[:, 1]
    code = left * 512 + right
    target = jnp.arange(NC, dtype=jnp.int32)[:, None]
    mine = live[None] & (pairs[:, 2][None] == target)
    seat = jnp.sum(mine[:, None, :] & (flat[None, None, :] < flat[None, :, None]), axis=-1)
    hit = mine[:, :, None] & (seat[:, :, None] == flat[None, None, :])
    listed = jnp.sum(jnp.where(hit, code[None, :, None] - ZERO, 0), axis=1) + ZERO
    return listed.astype(jnp.int32), jnp.sum(mine, axis=1).astype(jnp.int32)


def product_kernel(plan, codes, counts, *refs):
    pieces, (out, held, sems) = refs[:-3], refs[-3:]
    copies = []
    for piece, (size, at) in zip(pieces, plan, strict=True):
        copies.append(
            pltpu.make_async_copy(piece, held.at[pl.ds(at, size)], sems.at[len(copies)])
        )
    for copy in copies:
        copy.start()
    held[ZERO] = jnp.zeros((BS, BS), jnp.bfloat16)
    for copy in copies:
        copy.wait()

    def part(n, step):
        first, second = [], []
        for g in range(GROUP):
            code = codes[n, step * GROUP + g]
            first.append(held[code // 512])
            second.append(held[code % 512])
        return jnp.dot(
            jnp.concatenate(first, axis=1),
            jnp.concatenate(second, axis=0),
            preferred_element_type=jnp.float32,
        )

    steps = (jnp.maximum(counts[0], counts[1]) + GROUP - 1) // GROUP
    zero = jnp.zeros((BS, BS), jnp.float32)

    def step(turn, total):
        return total[0] + part(0, turn), total[1] + part(1, turn)

    total = lax.fori_loop(0, steps, step, (zero, zero))
    out[0] = total[0].astype(jnp.bfloat16)
    out[1] = total[1].astype(jnp.bfloat16)


def along_plane(value, shift):
    pairs = []
    for x in range(NX):
        for y in range(NY):
            place = (x * NY + y) * NCORE
            pairs.append((place, ((x + shift) % NX * NY + y) * NCORE))
            pairs.append((place + 1, (x * NY + (y + shift) % NY) * NCORE + 1))
    return lax.ppermute(value, ("x", "y", "c"), pairs)


def along_z(value, shift, swap):
    pairs = []
    for zl in range(NZL):
        for zh in range(NZH):
            place = (zl * NZH + zh) * NCORE
            pairs.append((place, ((zl + shift) % NZL * NZH + zh) * NCORE))
            pairs.append((place + 1, (zl * NZH + (zh + swap) % NZH) * NCORE + 1))
    return lax.ppermute(value, ("zl", "zh", "c"), pairs)


def to_partner(value):
    return lax.ppermute(value, "c", rot(NCORE, 1))


def per_device(left_blocks, right_blocks, pair_lists, pair_count):
    x, zl, zh, y, c = (lax.axis_index(name) for name in ("x", "zl", "zh", "y", "c"))

    got = to_partner(jnp.where(c == 0, left_blocks, jnp.concatenate([right_blocks] * 2)))
    rights = jnp.concatenate([right_blocks, got[:NB]])
    first, second = jnp.where(c == 0, rights, got), jnp.where(c == 0, rights, left_blocks)
    own = jnp.concatenate(
        [first, along_z(first, 1, 1), along_z(second, 2, 1), along_z(second, 3, 0)]
    )
    half = TILE // 2
    behind, ahead = along_plane(own, 2), along_plane(own, -2)
    near = [own, along_plane(own, 1), along_plane(own, -1)]
    far = [along_plane(behind[:half], 2), along_plane(ahead[half:], -2)]
    pieces = [jnp.concatenate(near), jnp.concatenate([behind, ahead])]
    pieces += [along_plane(behind, 1), along_plane(ahead, -1), jnp.concatenate(far)]
    pieces += [to_partner(piece) for piece in pieces]
    plan, at = [], 0
    for piece in pieces:
        plan.append((piece.shape[0], at))
        at += piece.shape[0]

    codes, counts = slot_lists(pair_lists, pair_count, x, zl, zh, y, c)

    def kernel(*refs):
        product_kernel(plan, *refs)

    return pl.pallas_call(
        kernel,
        out_shape=jax.ShapeDtypeStruct((NC, BS, BS), jnp.bfloat16),
        in_specs=[pl.BlockSpec(memory_space=pltpu.SMEM)] * 2
        + [pl.BlockSpec(memory_space=pl.ANY)] * len(pieces),
        out_specs=pl.BlockSpec(memory_space=pltpu.VMEM),
        scratch_shapes=[
            pltpu.VMEM((ZERO + 1, BS, BS), jnp.bfloat16),
            pltpu.SemaphoreType.DMA((len(plan),)),
        ],
        compiler_params=pltpu.CompilerParams(vmem_limit_bytes=16 * 1024 * 1024),
        cost_estimate=pl.CostEstimate(
            flops=2 * 128 * BS**3, bytes_accessed=6 * 1024 * 1024, transcendentals=0
        ),
        name="block_products",
    )(codes, counts, *pieces)


def solution(mesh):
    parts = Mesh(mesh.devices.reshape(NX, NZL, NZH, NY, NCORE), ("x", "zl", "zh", "y", "c"))
    row, col = ("x", "zl"), ("zh", "y", "c")
    return jax.shard_map(
        per_device,
        mesh=parts,
        in_specs=(P(row, col, None), P(col, row, None), P(row + col, None, None), P(row + col, None)),
        out_specs=P(row + col, None, None),
        check_vma=False,
    )
```

```python
import jax
import jax.numpy as jnp
from jax import lax
from jax.experimental import pallas as pl
from jax.experimental.pallas import tpu as pltpu
from jax.sharding import Mesh
from jax.sharding import PartitionSpec as P

NX, NZL, NZH, NY, NCORE = 8, 4, 2, 8, 2
NK = 32
NA, NB, NC, NT = 4, 2, 2, 8
BS = 128
GROUP = 16
TILE = 16
ZERO = 2 * NY * TILE
SEATS = (1, 4, 7, 2, 5, 0, 3, 6)


def rot(size, shift):
    return [(s, (s + shift) % size) for s in range(size)]


def seat_of(distance):
    hit = distance[:, None] % NY == jnp.arange(NY, dtype=jnp.int32)
    return jnp.sum(jnp.where(hit, jnp.array(SEATS, jnp.int32), 0), axis=1)


def slot_lists(pair_lists, pair_count, x, zl, zh, y, c):
    pairs = pair_lists.reshape(NK * NT, 3)
    flat = jnp.arange(NK * NT, dtype=jnp.int32)
    k = flat // NT
    live = flat % NT < jnp.repeat(pair_count.reshape(NK), NT)
    row, col = x * NZL + zl, (zh * NY + y) * NCORE + c
    source = (k - row) % NK
    from_zh, from_y, from_c = source // (NY * NCORE), source // NCORE % NY, source % NCORE
    near = from_zh == zh
    part = jnp.where(from_c == 0, jnp.where(near, 0, 1), jnp.where(near, 3, 2))
    left = (jnp.where(c == 1, 0, NY) + seat_of(from_y - y)) * TILE + part * NA + pairs[:, 0]
    holder = (k - col) % NK
    part = (zl - holder % NZL) % NZL
    right = (jnp.where(c == 0, 0, NY) + seat_of(holder // NZL - x)) * TILE
    right = right + (part * NCORE + c) * NB + pairs[:, 1]
    code = left * 512 + right
    target = jnp.arange(NC, dtype=jnp.int32)[:, None]
    mine = live[None] & (pairs[:, 2][None] == target)
    seat = jnp.sum(mine[:, None, :] & (flat[None, None, :] < flat[None, :, None]), axis=-1)
    hit = mine[:, :, None] & (seat[:, :, None] == flat[None, None, :])
    listed = jnp.sum(jnp.where(hit, code[None, :, None] - ZERO, 0), axis=1) + ZERO
    return listed.astype(jnp.int32), jnp.sum(mine, axis=1).astype(jnp.int32)


def product_kernel(plan, codes, counts, *refs):
    pieces, (out, held, sems) = refs[:-3], refs[-3:]
    copies = []
    for piece, (size, at) in zip(pieces, plan, strict=True):
        copies.append(
            pltpu.make_async_copy(piece, held.at[pl.ds(at, size)], sems.at[len(copies)])
        )
    for copy in copies:
        copy.start()
    held[ZERO] = jnp.zeros((BS, BS), jnp.bfloat16)
    for copy in copies:
        copy.wait()

    def part(n, step):
        first, second = [], []
        for g in range(GROUP):
            code = codes[n, step * GROUP + g]
            first.append(held[code // 512])
            second.append(held[code % 512])
        return jnp.dot(
            jnp.concatenate(first, axis=1),
            jnp.concatenate(second, axis=0),
            preferred_element_type=jnp.float32,
        )

    steps = (jnp.maximum(counts[0], counts[1]) + GROUP - 1) // GROUP
    zero = jnp.zeros((BS, BS), jnp.float32)

    def step(turn, total):
        return total[0] + part(0, turn), total[1] + part(1, turn)

    total = lax.fori_loop(0, steps, step, (zero, zero))
    out[0] = total[0].astype(jnp.bfloat16)
    out[1] = total[1].astype(jnp.bfloat16)


def along_plane(value, shift):
    pairs = []
    for x in range(NX):
        for y in range(NY):
            place = (x * NY + y) * NCORE
            pairs.append((place, ((x + shift) % NX * NY + y) * NCORE))
            pairs.append((place + 1, (x * NY + (y + shift) % NY) * NCORE + 1))
    return lax.ppermute(value, ("x", "y", "c"), pairs)


def along_z(value, shift, swap):
    pairs = []
    for zl in range(NZL):
        for zh in range(NZH):
            place = (zl * NZH + zh) * NCORE
            pairs.append((place, ((zl + shift) % NZL * NZH + zh) * NCORE))
            pairs.append((place + 1, (zl * NZH + (zh + swap) % NZH) * NCORE + 1))
    return lax.ppermute(value, ("zl", "zh", "c"), pairs)


def to_partner(value):
    return lax.ppermute(value, "c", rot(NCORE, 1))


def per_device(left_blocks, right_blocks, pair_lists, pair_count):
    x, zl, zh, y, c = (lax.axis_index(name) for name in ("x", "zl", "zh", "y", "c"))

    got = to_partner(jnp.where(c == 0, left_blocks, jnp.concatenate([right_blocks] * 2)))
    rights = jnp.concatenate([right_blocks, got[:NB]])
    first, second = jnp.where(c == 0, rights, got), jnp.where(c == 0, rights, left_blocks)
    own = jnp.concatenate(
        [first, along_z(first, 1, 1), along_z(second, 2, 1), along_z(second, 3, 0)]
    )
    half = TILE // 2
    near = jnp.concatenate([along_plane(own, 3), own, along_plane(own, -3)])
    pieces = [near, along_plane(near[: 2 * TILE + half], -1), along_plane(near[half:], 1)]
    pieces += [to_partner(piece) for piece in pieces]
    plan, at = [], 0
    for piece in pieces:
        plan.append((piece.shape[0], at))
        at += piece.shape[0]

    codes, counts = slot_lists(pair_lists, pair_count, x, zl, zh, y, c)

    def kernel(*refs):
        product_kernel(plan, *refs)

    return pl.pallas_call(
        kernel,
        out_shape=jax.ShapeDtypeStruct((NC, BS, BS), jnp.bfloat16),
        in_specs=[pl.BlockSpec(memory_space=pltpu.SMEM)] * 2
        + [pl.BlockSpec(memory_space=pl.ANY)] * len(pieces),
        out_specs=pl.BlockSpec(memory_space=pltpu.VMEM),
        scratch_shapes=[
            pltpu.VMEM((ZERO + 1, BS, BS), jnp.bfloat16),
            pltpu.SemaphoreType.DMA((len(plan),)),
        ],
        compiler_params=pltpu.CompilerParams(vmem_limit_bytes=16 * 1024 * 1024),
        cost_estimate=pl.CostEstimate(
            flops=2 * 128 * BS**3, bytes_accessed=6 * 1024 * 1024, transcendentals=0
        ),
        name="block_products",
    )(codes, counts, *pieces)


def solution(mesh):
    parts = Mesh(mesh.devices.reshape(NX, NZL, NZH, NY, NCORE), ("x", "zl", "zh", "y", "c"))
    row, col = ("x", "zl"), ("zh", "y", "c")
    return jax.shard_map(
        per_device,
        mesh=parts,
        in_specs=(P(row, col, None), P(col, row, None), P(row + col, None, None), P(row + col, None)),
        out_specs=P(row + col, None, None),
        check_vma=False,
    )
```

```python
import jax
import jax.numpy as jnp
from jax import lax
from jax.experimental import pallas as pl
from jax.experimental.pallas import tpu as pltpu
from jax.sharding import Mesh
from jax.sharding import PartitionSpec as P

NX, NZL, NZH, NY, NCORE = 8, 4, 2, 8, 2
NK = 32
NA, NB, NC, NT = 4, 2, 2, 8
BS = 128
GROUP = 16
TILE = 8
ZERO = 3 * NY * TILE
SEATS = (1, 5, 2, 6, 7, 3, 0, 4)


def rot(size, shift):
    return [(s, (s + shift) % size) for s in range(size)]


def seat_of(distance):
    hit = distance[:, None] % NY == jnp.arange(NY, dtype=jnp.int32)
    return jnp.sum(jnp.where(hit, jnp.array(SEATS, jnp.int32), 0), axis=1)


def slot_lists(pair_lists, pair_count, x, zl, col, c):
    pairs = pair_lists.reshape(NK * NT, 3)
    flat = jnp.arange(NK * NT, dtype=jnp.int32)
    k = flat // NT
    live = flat % NT < jnp.repeat(pair_count.reshape(NK), NT)
    row = x * NZL + zl
    source = (k - row) % NK
    left = jnp.where(source % NCORE == c, 0, NY * TILE) + source // NCORE * NA + pairs[:, 0]
    holder = (k - col) % NK
    right = (2 * NY + seat_of(holder // NZL - x)) * TILE
    right = right + (zl - holder % NZL) % NZL * NB + pairs[:, 1]
    code = left * 256 + right
    target = jnp.arange(NC, dtype=jnp.int32)[:, None]
    mine = live[None] & (pairs[:, 2][None] == target)
    seat = jnp.sum(mine[:, None, :] & (flat[None, None, :] < flat[None, :, None]), axis=-1)
    hit = mine[:, :, None] & (seat[:, :, None] == flat[None, None, :])
    listed = jnp.sum(jnp.where(hit, code[None, :, None] - ZERO, 0), axis=1) + ZERO
    return listed.astype(jnp.int32), jnp.sum(mine, axis=1).astype(jnp.int32)


def product_kernel(plan, codes, counts, *refs):
    pieces, (out, held, sems) = refs[:-3], refs[-3:]
    copies = []
    for piece, (size, at) in zip(pieces, plan, strict=True):
        copies.append(
            pltpu.make_async_copy(piece, held.at[pl.ds(at, size)], sems.at[len(copies)])
        )
    for copy in copies:
        copy.start()
    held[ZERO] = jnp.zeros((BS, BS), jnp.bfloat16)
    for copy in copies:
        copy.wait()

    def part(n, step):
        first, second = [], []
        for g in range(GROUP):
            code = codes[n, step * GROUP + g]
            first.append(held[code // 256])
            second.append(held[code % 256])
        return jnp.dot(
            jnp.concatenate(first, axis=1),
            jnp.concatenate(second, axis=0),
            preferred_element_type=jnp.float32,
        )

    steps = (jnp.maximum(counts[0], counts[1]) + GROUP - 1) // GROUP
    zero = jnp.zeros((BS, BS), jnp.float32)

    def step(turn, total):
        return total[0] + part(0, turn), total[1] + part(1, turn)

    total = lax.fori_loop(0, steps, step, (zero, zero))
    out[0] = total[0].astype(jnp.bfloat16)
    out[1] = total[1].astype(jnp.bfloat16)


def per_device(left_blocks, right_blocks, pair_lists, pair_count):
    x, zl, zh, y, c = (lax.axis_index(name) for name in ("x", "zl", "zh", "y", "c"))
    col = (zh * NY + y) * NCORE + c
    codes, counts = slot_lists(pair_lists, pair_count, x, zl, col, c)

    own = [right_blocks]
    own += [lax.ppermute(right_blocks, "zl", rot(NZL, shift)) for shift in range(1, NZL)]
    left_blocks, *own = lax.optimization_barrier((left_blocks, *own))
    spread = jnp.broadcast_to(left_blocks[None], (NZH * NY,) + left_blocks.shape)
    lefts = spread.reshape(NZH * NY * NA, BS, BS)
    lefts = lax.all_to_all(lefts, ("zh", "y"), 0, 0, tiled=True)

    own = jnp.concatenate(own)
    half = TILE // 2
    behind = lax.ppermute(own, "x", rot(NX, 2))
    ahead = lax.ppermute(own, "x", rot(NX, -2))
    behind, ahead, codes, counts = lax.optimization_barrier((behind, ahead, codes, counts))
    near = jnp.concatenate([behind, own, ahead])
    rights = [near]
    rights.append(lax.ppermute(near[: 2 * TILE], "x", rot(NX, 1)))
    rights.append(lax.ppermute(near[TILE:], "x", rot(NX, -1)))
    rights.append(lax.ppermute(behind[:half], "x", rot(NX, 2)))
    rights.append(lax.ppermute(ahead[half:], "x", rot(NX, -2)))

    lefts, *rights = lax.optimization_barrier((lefts, *rights))
    pieces = [lefts, lax.ppermute(lefts, "c", rot(NCORE, 1))] + rights
    plan, at = [], 0
    for piece in pieces:
        plan.append((piece.shape[0], at))
        at += piece.shape[0]

    def kernel(*refs):
        product_kernel(plan, *refs)

    return pl.pallas_call(
        kernel,
        out_shape=jax.ShapeDtypeStruct((NC, BS, BS), jnp.bfloat16),
        in_specs=[pl.BlockSpec(memory_space=pltpu.SMEM)] * 2
        + [pl.BlockSpec(memory_space=pl.ANY)] * len(pieces),
        out_specs=pl.BlockSpec(memory_space=pltpu.VMEM),
        scratch_shapes=[
            pltpu.VMEM((ZERO + 1, BS, BS), jnp.bfloat16),
            pltpu.SemaphoreType.DMA((len(plan),)),
        ],
        compiler_params=pltpu.CompilerParams(vmem_limit_bytes=16 * 1024 * 1024),
        cost_estimate=pl.CostEstimate(
            flops=2 * 128 * BS**3, bytes_accessed=6 * 1024 * 1024, transcendentals=0
        ),
        name="block_products",
    )(codes, counts, *pieces)


def solution(mesh):
    parts = Mesh(mesh.devices.reshape(NX, NZL, NZH, NY, NCORE), ("x", "zl", "zh", "y", "c"))
    row, col = ("x", "zl"), ("zh", "y", "c")
    return jax.shard_map(
        per_device,
        mesh=parts,
        in_specs=(P(row, col, None), P(col, row, None), P(row + col, None, None), P(row + col, None)),
        out_specs=P(row + col, None, None),
        check_vma=False,
    )
```

```python
import jax
import jax.numpy as jnp
from jax import lax
from jax.experimental import pallas as pl
from jax.experimental.pallas import tpu as pltpu
from jax.sharding import Mesh
from jax.sharding import PartitionSpec as P

NX, NZL, NZH, NY, NCORE = 8, 4, 2, 8, 2
NK = 32
NA, NB, NC, NT = 4, 2, 2, 8
BS = 128
GROUP = 16
TILE = 16
ZERO = 2 * NY * TILE


def rot(size, shift):
    return [(s, (s + shift) % size) for s in range(size)]


def slot_lists(pair_lists, pair_count, x, zl, zh, y, c):
    pairs = pair_lists.reshape(NK * NT, 3)
    flat = jnp.arange(NK * NT, dtype=jnp.int32)
    k = flat // NT
    live = flat % NT < jnp.repeat(pair_count.reshape(NK), NT)
    row, col = x * NZL + zl, (zh * NY + y) * NCORE + c
    source = (k - row) % NK
    from_zh, from_y, from_c = source // (NY * NCORE), source // NCORE % NY, source % NCORE
    near = from_zh == zh
    part = jnp.where(from_c == 0, jnp.where(near, 0, 1), jnp.where(near, 3, 2))
    left = (jnp.where(c == 1, 0, NY) + (from_y - y) * (1 - y % 2 * 2) % NY) * TILE + part * NA + pairs[:, 0]
    holder = (k - col) % NK
    part = zl ^ holder % NZL
    right = (jnp.where(c == 0, 0, NY) + (holder // NZL - x) * (1 - x % 2 * 2) % NX) * TILE
    right = right + (part * NCORE + c) * NB + pairs[:, 1]
    code = left * 512 + right
    target = jnp.arange(NC, dtype=jnp.int32)[:, None]
    mine = live[None] & (pairs[:, 2][None] == target)
    seat = jnp.sum(mine[:, None, :] & (flat[None, None, :] < flat[None, :, None]), axis=-1)
    hit = mine[:, :, None] & (seat[:, :, None] == flat[None, None, :])
    listed = jnp.sum(jnp.where(hit, code[None, :, None] - ZERO, 0), axis=1) + ZERO
    return listed.astype(jnp.int32), jnp.sum(mine, axis=1).astype(jnp.int32)


def product_kernel(plan, codes, counts, *refs):
    pieces, (out, held, sems) = refs[:-3], refs[-3:]
    copies = []
    for piece, (size, at) in zip(pieces, plan, strict=True):
        copies.append(
            pltpu.make_async_copy(piece, held.at[pl.ds(at, size)], sems.at[len(copies)])
        )
    for copy in copies:
        copy.start()
    held[ZERO] = jnp.zeros((BS, BS), jnp.bfloat16)
    for copy in copies:
        copy.wait()

    def part(n, step):
        first, second = [], []
        for g in range(GROUP):
            code = codes[n, step * GROUP + g]
            first.append(held[code // 512])
            second.append(held[code % 512])
        return jnp.dot(
            jnp.concatenate(first, axis=1),
            jnp.concatenate(second, axis=0),
            preferred_element_type=jnp.float32,
        )

    steps = (jnp.maximum(counts[0], counts[1]) + GROUP - 1) // GROUP
    zero = jnp.zeros((BS, BS), jnp.float32)

    def step(turn, total):
        return total[0] + part(0, turn), total[1] + part(1, turn)

    total = lax.fori_loop(0, steps, step, (zero, zero))
    out[0] = total[0].astype(jnp.bfloat16)
    out[1] = total[1].astype(jnp.bfloat16)


def along_plane(value, kind):
    pairs = []
    for x in range(NX):
        for y in range(NY):
            place = (x * NY + y) * NCORE
            pairs.append((place, ((((x + kind) ^ 1) - kind) % NX * NY + y) * NCORE))
            pairs.append((place + 1, (x * NY + (((y + kind) ^ 1) - kind) % NY) * NCORE + 1))
    return lax.ppermute(value, ("x", "y", "c"), pairs)


def along_z(value, flip, swap):
    pairs = []
    for zl in range(NZL):
        for zh in range(NZH):
            place = (zl * NZH + zh) * NCORE
            pairs.append((place, ((zl ^ flip) * NZH + zh) * NCORE))
            pairs.append((place + 1, (zl * NZH + (zh + swap) % NZH) * NCORE + 1))
    return lax.ppermute(value, ("zl", "zh", "c"), pairs)


def to_partner(value):
    return lax.ppermute(value, "c", rot(NCORE, 1))


def per_device(left_blocks, right_blocks, pair_lists, pair_count):
    x, zl, zh, y, c = (lax.axis_index(name) for name in ("x", "zl", "zh", "y", "c"))

    got = to_partner(jnp.where(c == 0, left_blocks, jnp.concatenate([right_blocks] * 2)))
    rights = jnp.concatenate([right_blocks, got[:NB]])
    first, second = jnp.where(c == 0, rights, got), jnp.where(c == 0, rights, left_blocks)
    own = jnp.concatenate(
        [first, along_z(first, 1, 1), along_z(second, 2, 1), along_z(second, 3, 0)]
    )
    half = TILE // 2
    pieces, plan = [own], [(TILE, 0)]
    one = two = own
    for distance in range(1, NY // 2):
        one, two = along_plane(two, 0), along_plane(one, 1)
        pieces += [one, two]
        plan += [(TILE, distance * TILE), (TILE, (NY - distance) * TILE)]
    pieces += [along_plane(two[:half], 0), along_plane(one[half:], 1)]
    plan += [(half, NY // 2 * TILE), (half, NY // 2 * TILE + half)]
    pieces += [to_partner(piece) for piece in pieces]
    plan += [(size, NY * TILE + at) for size, at in plan]

    codes, counts = slot_lists(pair_lists, pair_count, x, zl, zh, y, c)

    def kernel(*refs):
        product_kernel(plan, *refs)

    return pl.pallas_call(
        kernel,
        out_shape=jax.ShapeDtypeStruct((NC, BS, BS), jnp.bfloat16),
        in_specs=[pl.BlockSpec(memory_space=pltpu.SMEM)] * 2
        + [pl.BlockSpec(memory_space=pl.ANY)] * len(pieces),
        out_specs=pl.BlockSpec(memory_space=pltpu.VMEM),
        scratch_shapes=[
            pltpu.VMEM((ZERO + 1, BS, BS), jnp.bfloat16),
            pltpu.SemaphoreType.DMA((len(plan),)),
        ],
        compiler_params=pltpu.CompilerParams(vmem_limit_bytes=16 * 1024 * 1024),
        cost_estimate=pl.CostEstimate(
            flops=2 * 128 * BS**3, bytes_accessed=6 * 1024 * 1024, transcendentals=0
        ),
        name="block_products",
    )(codes, counts, *pieces)


def solution(mesh):
    parts = Mesh(mesh.devices.reshape(NX, NZL, NZH, NY, NCORE), ("x", "zl", "zh", "y", "c"))
    row, col = ("x", "zl"), ("zh", "y", "c")
    return jax.shard_map(
        per_device,
        mesh=parts,
        in_specs=(P(row, col, None), P(col, row, None), P(row + col, None, None), P(row + col, None)),
        out_specs=P(row + col, None, None),
        check_vma=False,
    )
```

```python
import jax
import jax.numpy as jnp
from jax import lax
from jax.experimental import pallas as pl
from jax.experimental.pallas import tpu as pltpu
from jax.sharding import Mesh
from jax.sharding import PartitionSpec as P

NX, NZL, NZH, NY, NCORE = 8, 4, 2, 8, 2
NK = 32
NA, NB, NC, NT = 4, 2, 2, 8
BS = 128
GROUP = 16
TILE = 8
ZERO = 3 * NY * TILE
SEATS = (0, 1, 3, 5, 7, 6, 4, 2)


def rot(size, shift):
    return [(s, (s + shift) % size) for s in range(size)]


def seat_of(distance):
    hit = distance[:, None] % NY == jnp.arange(NY, dtype=jnp.int32)
    return jnp.sum(jnp.where(hit, jnp.array(SEATS, jnp.int32), 0), axis=1)


def slot_lists(pair_lists, pair_count, x, zl, zh, y, c):
    pairs = pair_lists.reshape(NK * NT, 3)
    flat = jnp.arange(NK * NT, dtype=jnp.int32)
    k = flat // NT
    live = flat % NT < jnp.repeat(pair_count.reshape(NK), NT)
    row, col = x * NZL + zl, (zh * NY + y) * NCORE + c
    source = (k - row) % NK
    from_zh, from_y, from_c = source // (NY * NCORE), source // NCORE % NY, source % NCORE
    left = (jnp.where(from_c == c, 0, NY) + seat_of((from_y - y) * (1 - y % 2 * 2))) * TILE + pairs[:, 0]
    left = left + jnp.where(from_zh == zh, 0, NA)
    holder = (k - col) % NK
    right = (2 * NY + seat_of((holder // NZL - x) * (1 - x % 2 * 2))) * TILE
    right = right + (zl ^ holder % NZL) * NB + pairs[:, 1]
    code = left * 256 + right
    target = jnp.arange(NC, dtype=jnp.int32)[:, None]
    mine = live[None] & (pairs[:, 2][None] == target)
    seat = jnp.sum(mine[:, None, :] & (flat[None, None, :] < flat[None, :, None]), axis=-1)
    hit = mine[:, :, None] & (seat[:, :, None] == flat[None, None, :])
    listed = jnp.sum(jnp.where(hit, code[None, :, None] - ZERO, 0), axis=1) + ZERO
    return listed.astype(jnp.int32), jnp.sum(mine, axis=1).astype(jnp.int32)


def product_kernel(plan, codes, counts, *refs):
    pieces, (out, held, sems) = refs[:-3], refs[-3:]
    copies = []
    for piece, (size, at) in zip(pieces, plan, strict=True):
        copies.append(
            pltpu.make_async_copy(piece, held.at[pl.ds(at, size)], sems.at[len(copies)])
        )
    for copy in copies:
        copy.start()
    held[ZERO] = jnp.zeros((BS, BS), jnp.bfloat16)
    for copy in copies:
        copy.wait()

    def part(n, step):
        first, second = [], []
        for g in range(GROUP):
            code = codes[n, step * GROUP + g]
            first.append(held[code // 256])
            second.append(held[code % 256])
        return jnp.dot(
            jnp.concatenate(first, axis=1),
            jnp.concatenate(second, axis=0),
            preferred_element_type=jnp.float32,
        )

    steps = (jnp.maximum(counts[0], counts[1]) + GROUP - 1) // GROUP
    zero = jnp.zeros((BS, BS), jnp.float32)

    def step(turn, total):
        return total[0] + part(0, turn), total[1] + part(1, turn)

    total = lax.fori_loop(0, steps, step, (zero, zero))
    out[0] = total[0].astype(jnp.bfloat16)
    out[1] = total[1].astype(jnp.bfloat16)


def swaps(size, kind):
    return [(s, (((s + kind) ^ 1) - kind) % size) for s in range(size)]


def ring(own, axis):
    pieces = [own]
    one = two = own
    for _ in range(1, NY // 2):
        one, two = lax.ppermute(two, axis, swaps(NY, 0)), lax.ppermute(one, axis, swaps(NY, 1))
        pieces += [one, two]
    half = TILE // 2
    pieces.append(lax.ppermute(two[:half], axis, swaps(NY, 0)))
    pieces.append(lax.ppermute(one[half:], axis, swaps(NY, 1)))
    return pieces


def per_device(left_blocks, right_blocks, pair_lists, pair_count):
    x, zl, zh, y, c = (lax.axis_index(name) for name in ("x", "zl", "zh", "y", "c"))

    own = [right_blocks]
    for flip in range(1, NZL):
        own.append(lax.ppermute(right_blocks, "zl", [(s, s ^ flip) for s in range(NZL)]))
    rights = ring(jnp.concatenate(own), "x")
    other = lax.ppermute(left_blocks, "zh", rot(NZH, 1))
    lefts = ring(jnp.concatenate([left_blocks, other]), "y")
    lefts = [jnp.concatenate(part) for part in (lefts[:3], lefts[3:5], lefts[5:])]
    pieces = lefts + [lax.ppermute(part, "c", rot(NCORE, 1)) for part in lefts] + rights
    plan, at = [], 0
    for piece in pieces:
        plan.append((piece.shape[0], at))
        at += piece.shape[0]

    codes, counts = slot_lists(pair_lists, pair_count, x, zl, zh, y, c)

    def kernel(*refs):
        product_kernel(plan, *refs)

    return pl.pallas_call(
        kernel,
        out_shape=jax.ShapeDtypeStruct((NC, BS, BS), jnp.bfloat16),
        in_specs=[pl.BlockSpec(memory_space=pltpu.SMEM)] * 2
        + [pl.BlockSpec(memory_space=pl.ANY)] * len(pieces),
        out_specs=pl.BlockSpec(memory_space=pltpu.VMEM),
        scratch_shapes=[
            pltpu.VMEM((ZERO + 1, BS, BS), jnp.bfloat16),
            pltpu.SemaphoreType.DMA((len(plan),)),
        ],
        compiler_params=pltpu.CompilerParams(vmem_limit_bytes=16 * 1024 * 1024),
        cost_estimate=pl.CostEstimate(
            flops=2 * 128 * BS**3, bytes_accessed=6 * 1024 * 1024, transcendentals=0
        ),
        name="block_products",
    )(codes, counts, *pieces)


def solution(mesh):
    parts = Mesh(mesh.devices.reshape(NX, NZL, NZH, NY, NCORE), ("x", "zl", "zh", "y", "c"))
    row, col = ("x", "zl"), ("zh", "y", "c")
    return jax.shard_map(
        per_device,
        mesh=parts,
        in_specs=(P(row, col, None), P(col, row, None), P(row + col, None, None), P(row + col, None)),
        out_specs=P(row + col, None, None),
        check_vma=False,
    )
```

```python
import jax
import jax.numpy as jnp
from jax import lax
from jax.experimental import pallas as pl
from jax.experimental.pallas import tpu as pltpu
from jax.sharding import Mesh
from jax.sharding import PartitionSpec as P

NX, NZL, NZH, NY, NCORE = 8, 4, 2, 8, 2
NK = 32
NA, NB, NC, NT = 4, 2, 2, 8
BS = 128
GROUP = 16
TILE = 16
ZERO = 2 * NY * TILE
SEATS = (1, 3, 0, 4, 7, 6, 2, 5)


def rot(size, shift):
    return [(s, (s + shift) % size) for s in range(size)]


def seat_of(distance, place):
    odd, even = 1 - place % 2 * 2, 1 - place // 2 % 2 * 2
    distance = distance * jnp.where(distance % 2 == 1, odd, even) % NY
    hit = distance[:, None] == jnp.arange(NY, dtype=jnp.int32)
    return jnp.sum(jnp.where(hit, jnp.array(SEATS, jnp.int32), 0), axis=1)


def slot_lists(pair_lists, pair_count, x, zl, zh, y, c):
    pairs = pair_lists.reshape(NK * NT, 3)
    flat = jnp.arange(NK * NT, dtype=jnp.int32)
    k = flat // NT
    live = flat % NT < jnp.repeat(pair_count.reshape(NK), NT)
    row, col = x * NZL + zl, (zh * NY + y) * NCORE + c
    source = (k - row) % NK
    from_zh, from_y, from_c = source // (NY * NCORE), source // NCORE % NY, source % NCORE
    near = from_zh == zh
    part = jnp.where(from_c == 0, jnp.where(near, 0, 1), jnp.where(near, 3, 2))
    left = (jnp.where(c == 1, 0, NY) + seat_of(from_y - y, y)) * TILE + part * NA + pairs[:, 0]
    holder = (k - col) % NK
    part = zl ^ holder % NZL
    right = (jnp.where(c == 0, 0, NY) + seat_of(holder // NZL - x, x)) * TILE
    right = right + (part * NCORE + c) * NB + pairs[:, 1]
    code = left * 512 + right
    target = jnp.arange(NC, dtype=jnp.int32)[:, None]
    mine = live[None] & (pairs[:, 2][None] == target)
    seat = jnp.sum(mine[:, None, :] & (flat[None, None, :] < flat[None, :, None]), axis=-1)
    hit = mine[:, :, None] & (seat[:, :, None] == flat[None, None, :])
    listed = jnp.sum(jnp.where(hit, code[None, :, None] - ZERO, 0), axis=1) + ZERO
    return listed.astype(jnp.int32), jnp.sum(mine, axis=1).astype(jnp.int32)


def product_kernel(plan, codes, counts, *refs):
    pieces, (out, held, sems) = refs[:-3], refs[-3:]
    copies = []
    for piece, (size, at) in zip(pieces, plan, strict=True):
        copies.append(
            pltpu.make_async_copy(piece, held.at[pl.ds(at, size)], sems.at[len(copies)])
        )
    for copy in copies:
        copy.start()
    held[ZERO] = jnp.zeros((BS, BS), jnp.bfloat16)
    for copy in copies:
        copy.wait()

    def part(n, step):
        first, second = [], []
        for g in range(GROUP):
            code = codes[n, step * GROUP + g]
            first.append(held[code // 512])
            second.append(held[code % 512])
        return jnp.dot(
            jnp.concatenate(first, axis=1),
            jnp.concatenate(second, axis=0),
            preferred_element_type=jnp.float32,
        )

    steps = (jnp.maximum(counts[0], counts[1]) + GROUP - 1) // GROUP
    zero = jnp.zeros((BS, BS), jnp.float32)

    def step(turn, total):
        return total[0] + part(0, turn), total[1] + part(1, turn)

    total = lax.fori_loop(0, steps, step, (zero, zero))
    out[0] = total[0].astype(jnp.bfloat16)
    out[1] = total[1].astype(jnp.bfloat16)


def along_plane(value, reach, kind):
    pairs, shift = [], kind * reach
    for x in range(NX):
        for y in range(NY):
            place = (x * NY + y) * NCORE
            pairs.append((place, ((((x + shift) ^ reach) - shift) % NX * NY + y) * NCORE))
            to_y = (((y + shift) ^ reach) - shift) % NY
            pairs.append((place + 1, (x * NY + to_y) * NCORE + 1))
    return lax.ppermute(value, ("x", "y", "c"), pairs)


def along_z(value, flip, swap):
    pairs = []
    for zl in range(NZL):
        for zh in range(NZH):
            place = (zl * NZH + zh) * NCORE
            pairs.append((place, ((zl ^ flip) * NZH + zh) * NCORE))
            pairs.append((place + 1, (zl * NZH + (zh + swap) % NZH) * NCORE + 1))
    return lax.ppermute(value, ("zl", "zh", "c"), pairs)


def to_partner(value):
    return lax.ppermute(value, "c", rot(NCORE, 1))


def per_device(left_blocks, right_blocks, pair_lists, pair_count):
    x, zl, zh, y, c = (lax.axis_index(name) for name in ("x", "zl", "zh", "y", "c"))

    got = to_partner(jnp.where(c == 0, left_blocks, jnp.concatenate([right_blocks] * 2)))
    rights = jnp.concatenate([right_blocks, got[:NB]])
    first, second = jnp.where(c == 0, rights, got), jnp.where(c == 0, rights, left_blocks)
    own = jnp.concatenate(
        [first, along_z(first, 1, 1), along_z(second, 2, 1), along_z(second, 3, 0)]
    )
    half = TILE // 2
    one, two = along_plane(own, 2, 0), along_plane(own, 2, 1)
    place = jnp.where(c == 0, x, y)
    alike = place % 2 == place // 2 % 2
    pieces = [jnp.concatenate([one, own, two])]
    pieces.append(along_plane(jnp.concatenate([own, jnp.where(alike, two, one)]), 1, 0))
    pieces.append(along_plane(jnp.concatenate([own, jnp.where(alike, one, two)]), 1, 1))
    far = [along_plane(two[:half], 2, 0), along_plane(one[half:], 2, 1)]
    pieces.append(jnp.concatenate(far))
    pieces += [to_partner(piece) for piece in pieces]
    plan, at = [], 0
    for piece in pieces:
        plan.append((piece.shape[0], at))
        at += piece.shape[0]

    codes, counts = slot_lists(pair_lists, pair_count, x, zl, zh, y, c)

    def kernel(*refs):
        product_kernel(plan, *refs)

    return pl.pallas_call(
        kernel,
        out_shape=jax.ShapeDtypeStruct((NC, BS, BS), jnp.bfloat16),
        in_specs=[pl.BlockSpec(memory_space=pltpu.SMEM)] * 2
        + [pl.BlockSpec(memory_space=pl.ANY)] * len(pieces),
        out_specs=pl.BlockSpec(memory_space=pltpu.VMEM),
        scratch_shapes=[
            pltpu.VMEM((ZERO + 1, BS, BS), jnp.bfloat16),
            pltpu.SemaphoreType.DMA((len(plan),)),
        ],
        compiler_params=pltpu.CompilerParams(vmem_limit_bytes=16 * 1024 * 1024),
        cost_estimate=pl.CostEstimate(
            flops=2 * 128 * BS**3, bytes_accessed=6 * 1024 * 1024, transcendentals=0
        ),
        name="block_products",
    )(codes, counts, *pieces)


def solution(mesh):
    parts = Mesh(mesh.devices.reshape(NX, NZL, NZH, NY, NCORE), ("x", "zl", "zh", "y", "c"))
    row, col = ("x", "zl"), ("zh", "y", "c")
    return jax.shard_map(
        per_device,
        mesh=parts,
        in_specs=(P(row, col, None), P(col, row, None), P(row + col, None, None), P(row + col, None)),
        out_specs=P(row + col, None, None),
        check_vma=False,
    )
```

```python
import jax
import jax.numpy as jnp
from jax import lax
from jax.experimental import pallas as pl
from jax.experimental.pallas import tpu as pltpu
from jax.sharding import Mesh
from jax.sharding import PartitionSpec as P

NX, NZL, NZH, NY, NCORE = 8, 4, 2, 8, 2
NK = 32
NA, NB, NC, NT = 4, 2, 2, 8
BS = 128
GROUP = 16
TILE = 16
ZERO = 2 * NY * TILE
SEATS = (1, 5, 2, 6, 7, 3, 0, 4)


def rot(size, shift):
    return [(s, (s + shift) % size) for s in range(size)]


def seat_of(distance):
    hit = distance[:, None] % NY == jnp.arange(NY, dtype=jnp.int32)
    return jnp.sum(jnp.where(hit, jnp.array(SEATS, jnp.int32), 0), axis=1)


def slot_lists(pair_lists, pair_count, x, zl, zh, y, c):
    pairs = pair_lists.reshape(NK * NT, 3)
    flat = jnp.arange(NK * NT, dtype=jnp.int32)
    k = flat // NT
    live = flat % NT < jnp.repeat(pair_count.reshape(NK), NT)
    row, col = x * NZL + zl, (zh * NY + y) * NCORE + c
    source = (k - row) % NK
    from_zh, from_y, from_c = source // (NY * NCORE), source // NCORE % NY, source % NCORE
    near = from_zh == zh
    part = jnp.where(from_c == 0, jnp.where(near, 0, 1), jnp.where(near, 3, 2))
    left = (jnp.where(c == 1, 0, NY) + seat_of(from_y - y)) * TILE + part * NA + pairs[:, 0]
    holder = (k - col) % NK
    part = (zl - holder % NZL) % NZL
    right = (jnp.where(c == 0, 0, NY) + seat_of(holder // NZL - x)) * TILE
    right = right + (part * NCORE + c) * NB + pairs[:, 1]
    code = left * 512 + right
    target = jnp.arange(NC, dtype=jnp.int32)[:, None]
    mine = live[None] & (pairs[:, 2][None] == target)
    seat = jnp.sum(mine[:, None, :] & (flat[None, None, :] < flat[None, :, None]), axis=-1)
    hit = mine[:, :, None] & (seat[:, :, None] == flat[None, None, :])
    listed = jnp.sum(jnp.where(hit, code[None, :, None] - ZERO, 0), axis=1) + ZERO
    return listed.astype(jnp.int32), jnp.sum(mine, axis=1).astype(jnp.int32)


def product_kernel(plan, codes, counts, *refs):
    pieces, (out, held, sems) = refs[:-3], refs[-3:]
    copies = []
    for piece, (size, at) in zip(pieces, plan, strict=True):
        copies.append(
            pltpu.make_async_copy(piece, held.at[pl.ds(at, size)], sems.at[len(copies)])
        )
    for copy in copies:
        copy.start()
    held[ZERO] = jnp.zeros((BS, BS), jnp.bfloat16)
    for copy in copies:
        copy.wait()

    def part(n, step):
        first, second = [], []
        for g in range(GROUP):
            code = codes[n, step * GROUP + g]
            first.append(held[code // 512])
            second.append(held[code % 512])
        return jnp.dot(
            jnp.concatenate(first, axis=1),
            jnp.concatenate(second, axis=0),
            preferred_element_type=jnp.float32,
        )

    steps = (jnp.maximum(counts[0], counts[1]) + GROUP - 1) // GROUP
    zero = jnp.zeros((BS, BS), jnp.float32)

    def step(turn, total):
        return total[0] + part(0, turn), total[1] + part(1, turn)

    total = lax.fori_loop(0, steps, step, (zero, zero))
    out[0] = total[0].astype(jnp.bfloat16)
    out[1] = total[1].astype(jnp.bfloat16)


def along_plane(value, shift):
    pairs = []
    for x in range(NX):
        for y in range(NY):
            place = (x * NY + y) * NCORE
            pairs.append((place, ((x + shift) % NX * NY + y) * NCORE))
            pairs.append((place + 1, (x * NY + (y + shift) % NY) * NCORE + 1))
    return lax.ppermute(value, ("x", "y", "c"), pairs)


def along_z(value, shift, swap):
    pairs = []
    for zl in range(NZL):
        for zh in range(NZH):
            place = (zl * NZH + zh) * NCORE
            pairs.append((place, ((zl + shift) % NZL * NZH + zh) * NCORE))
            pairs.append((place + 1, (zl * NZH + (zh + swap) % NZH) * NCORE + 1))
    return lax.ppermute(value, ("zl", "zh", "c"), pairs)


def to_partner(value):
    return lax.ppermute(value, "c", rot(NCORE, 1))


def per_device(left_blocks, right_blocks, pair_lists, pair_count):
    x, zl, zh, y, c = (lax.axis_index(name) for name in ("x", "zl", "zh", "y", "c"))

    got = to_partner(jnp.where(c == 0, left_blocks, jnp.concatenate([right_blocks] * 2)))
    rights = jnp.concatenate([right_blocks, got[:NB]])
    first, second = jnp.where(c == 0, rights, got), jnp.where(c == 0, rights, left_blocks)
    own = jnp.concatenate(
        [first, along_z(first, 1, 1), along_z(second, 2, 1), along_z(second, 3, 0)]
    )
    own = lax.optimization_barrier(own)
    half = TILE // 2
    behind, ahead = along_plane(own, 2), along_plane(own, -2)
    near = jnp.concatenate([behind, own, ahead])
    pieces = [near, along_plane(near[: 2 * TILE], 1), along_plane(near[TILE:], -1)]
    far = [along_plane(behind[:half], 2), along_plane(ahead[half:], -2)]
    pieces.append(jnp.concatenate(far))
    pieces += [to_partner(piece) for piece in pieces]
    plan, at = [], 0
    for piece in pieces:
        plan.append((piece.shape[0], at))
        at += piece.shape[0]

    codes, counts = slot_lists(pair_lists, pair_count, x, zl, zh, y, c)

    def kernel(*refs):
        product_kernel(plan, *refs)

    return pl.pallas_call(
        kernel,
        out_shape=jax.ShapeDtypeStruct((NC, BS, BS), jnp.bfloat16),
        in_specs=[pl.BlockSpec(memory_space=pltpu.SMEM)] * 2
        + [pl.BlockSpec(memory_space=pl.ANY)] * len(pieces),
        out_specs=pl.BlockSpec(memory_space=pltpu.VMEM),
        scratch_shapes=[
            pltpu.VMEM((ZERO + 1, BS, BS), jnp.bfloat16),
            pltpu.SemaphoreType.DMA((len(plan),)),
        ],
        compiler_params=pltpu.CompilerParams(vmem_limit_bytes=16 * 1024 * 1024),
        cost_estimate=pl.CostEstimate(
            flops=2 * 128 * BS**3, bytes_accessed=6 * 1024 * 1024, transcendentals=0
        ),
        name="block_products",
    )(codes, counts, *pieces)


def solution(mesh):
    parts = Mesh(mesh.devices.reshape(NX, NZL, NZH, NY, NCORE), ("x", "zl", "zh", "y", "c"))
    row, col = ("x", "zl"), ("zh", "y", "c")
    return jax.shard_map(
        per_device,
        mesh=parts,
        in_specs=(P(row, col, None), P(col, row, None), P(row + col, None, None), P(row + col, None)),
        out_specs=P(row + col, None, None),
        check_vma=False,
    )
```

```python
import jax
import jax.numpy as jnp
from jax import lax
from jax.experimental import pallas as pl
from jax.experimental.pallas import tpu as pltpu
from jax.sharding import Mesh
from jax.sharding import PartitionSpec as P

NX, NZL, NZH, NY, NCORE = 8, 4, 2, 8, 2
NK = 32
NA, NB, NC, NT = 4, 2, 2, 8
BS = 128
GROUP = 16
TILE = 16
ZERO = 2 * NY * TILE
SEATS = (1, 5, 2, 6, 7, 3, 0, 4)


def rot(size, shift):
    return [(s, (s + shift) % size) for s in range(size)]


def seat_of(distance):
    hit = distance[:, None] % NY == jnp.arange(NY, dtype=jnp.int32)
    return jnp.sum(jnp.where(hit, jnp.array(SEATS, jnp.int32), 0), axis=1)


def slot_lists(pair_lists, pair_count, x, zl, zh, y, c):
    pairs = pair_lists.reshape(NK * NT, 3)
    flat = jnp.arange(NK * NT, dtype=jnp.int32)
    k = flat // NT
    live = flat % NT < jnp.repeat(pair_count.reshape(NK), NT)
    row, col = x * NZL + zl, (zh * NY + y) * NCORE + c
    source = (k - row) % NK
    from_zh, from_y, from_c = source // (NY * NCORE), source // NCORE % NY, source % NCORE
    near = from_zh == zh
    part = jnp.where(from_c == 0, jnp.where(near, 0, 1), jnp.where(near, 2, 3))
    left = (jnp.where(c == 1, 0, NY) + seat_of(from_y - y)) * TILE + part * NA + pairs[:, 0]
    holder = (k - col) % NK
    part = (zl - holder % NZL) % NZL
    part = part ^ part // 2
    right = (jnp.where(c == 0, 0, NY) + seat_of(holder // NZL - x)) * TILE
    right = right + (part * NCORE + c) * NB + pairs[:, 1]
    code = left * 512 + right
    target = jnp.arange(NC, dtype=jnp.int32)[:, None]
    mine = live[None] & (pairs[:, 2][None] == target)
    seat = jnp.sum(mine[:, None, :] & (flat[None, None, :] < flat[None, :, None]), axis=-1)
    hit = mine[:, :, None] & (seat[:, :, None] == flat[None, None, :])
    listed = jnp.sum(jnp.where(hit, code[None, :, None] - ZERO, 0), axis=1) + ZERO
    return listed.astype(jnp.int32), jnp.sum(mine, axis=1).astype(jnp.int32)


def product_kernel(plan, codes, counts, *refs):
    pieces, (out, held, sems) = refs[:-3], refs[-3:]
    copies = []
    for piece, (size, at) in zip(pieces, plan, strict=True):
        copies.append(
            pltpu.make_async_copy(piece, held.at[pl.ds(at, size)], sems.at[len(copies)])
        )
    for copy in copies:
        copy.start()
    held[ZERO] = jnp.zeros((BS, BS), jnp.bfloat16)
    for copy in copies:
        copy.wait()

    def part(n, step):
        first, second = [], []
        for g in range(GROUP):
            code = codes[n, step * GROUP + g]
            first.append(held[code // 512])
            second.append(held[code % 512])
        return jnp.dot(
            jnp.concatenate(first, axis=1),
            jnp.concatenate(second, axis=0),
            preferred_element_type=jnp.float32,
        )

    steps = (jnp.maximum(counts[0], counts[1]) + GROUP - 1) // GROUP
    zero = jnp.zeros((BS, BS), jnp.float32)

    def step(turn, total):
        return total[0] + part(0, turn), total[1] + part(1, turn)

    total = lax.fori_loop(0, steps, step, (zero, zero))
    out[0] = total[0].astype(jnp.bfloat16)
    out[1] = total[1].astype(jnp.bfloat16)


def along_plane(value, shift):
    pairs = []
    for x in range(NX):
        for y in range(NY):
            place = (x * NY + y) * NCORE
            pairs.append((place, ((x + shift) % NX * NY + y) * NCORE))
            pairs.append((place + 1, (x * NY + (y + shift) % NY) * NCORE + 1))
    return lax.ppermute(value, ("x", "y", "c"), pairs)


def along_z(value, shift, swap):
    pairs = []
    for zl in range(NZL):
        for zh in range(NZH):
            place = (zl * NZH + zh) * NCORE
            pairs.append((place, ((zl + shift) % NZL * NZH + zh) * NCORE))
            pairs.append((place + 1, (zl * NZH + (zh + swap) % NZH) * NCORE + 1))
    return lax.ppermute(value, ("zl", "zh", "c"), pairs)


def to_partner(value):
    return lax.ppermute(value, "c", rot(NCORE, 1))


def per_device(left_blocks, right_blocks, pair_lists, pair_count):
    x, zl, zh, y, c = (lax.axis_index(name) for name in ("x", "zl", "zh", "y", "c"))

    got = to_partner(jnp.where(c == 0, left_blocks, jnp.concatenate([right_blocks] * 2)))
    rights = jnp.concatenate([right_blocks, got[:NB]])
    first, second = jnp.where(c == 0, rights, got), jnp.where(c == 0, rights, left_blocks)
    own = jnp.concatenate(
        [first, along_z(first, 1, 1), along_z(second, 3, 0), along_z(second, 2, 1)]
    )
    own = lax.optimization_barrier(own)
    half = TILE // 2
    behind, ahead = along_plane(own, 2), along_plane(own, -2)
    near = jnp.concatenate([behind, own, ahead])
    pieces = [near, along_plane(near[: 2 * TILE], 1), along_plane(near[TILE:], -1)]
    far = [along_plane(behind[:half], 2), along_plane(ahead[half:], -2)]
    pieces.append(jnp.concatenate(far))
    pieces += [to_partner(piece) for piece in pieces]
    plan, at = [], 0
    for piece in pieces:
        plan.append((piece.shape[0], at))
        at += piece.shape[0]

    codes, counts = slot_lists(pair_lists, pair_count, x, zl, zh, y, c)

    def kernel(*refs):
        product_kernel(plan, *refs)

    return pl.pallas_call(
        kernel,
        out_shape=jax.ShapeDtypeStruct((NC, BS, BS), jnp.bfloat16),
        in_specs=[pl.BlockSpec(memory_space=pltpu.SMEM)] * 2
        + [pl.BlockSpec(memory_space=pl.ANY)] * len(pieces),
        out_specs=pl.BlockSpec(memory_space=pltpu.VMEM),
        scratch_shapes=[
            pltpu.VMEM((ZERO + 1, BS, BS), jnp.bfloat16),
            pltpu.SemaphoreType.DMA((len(plan),)),
        ],
        compiler_params=pltpu.CompilerParams(vmem_limit_bytes=16 * 1024 * 1024),
        cost_estimate=pl.CostEstimate(
            flops=2 * 128 * BS**3, bytes_accessed=6 * 1024 * 1024, transcendentals=0
        ),
        name="block_products",
    )(codes, counts, *pieces)


def solution(mesh):
    parts = Mesh(mesh.devices.reshape(NX, NZL, NZH, NY, NCORE), ("x", "zl", "zh", "y", "c"))
    row, col = ("x", "zl"), ("zh", "y", "c")
    return jax.shard_map(
        per_device,
        mesh=parts,
        in_specs=(P(row, col, None), P(col, row, None), P(row + col, None, None), P(row + col, None)),
        out_specs=P(row + col, None, None),
        check_vma=False,
    )
```

```python
import jax
import jax.numpy as jnp
from jax import lax
from jax.experimental import pallas as pl
from jax.experimental.pallas import tpu as pltpu
from jax.sharding import Mesh
from jax.sharding import PartitionSpec as P

NX, NZL, NZH, NY, NCORE = 8, 4, 2, 8, 2
NK = 32
NA, NB, NC, NT = 4, 2, 2, 8
BS = 128
GROUP = 16
TILE = 16
ZERO = 2 * NY * TILE
SEATS = (0, 5, 2, 6, 7, 3, 1, 4)


def rot(size, shift):
    return [(s, (s + shift) % size) for s in range(size)]


def seat_of(distance):
    hit = distance[:, None] % NY == jnp.arange(NY, dtype=jnp.int32)
    return jnp.sum(jnp.where(hit, jnp.array(SEATS, jnp.int32), 0), axis=1)


def slot_lists(pair_lists, pair_count, x, zl, zh, y, c):
    pairs = pair_lists.reshape(NK * NT, 3)
    flat = jnp.arange(NK * NT, dtype=jnp.int32)
    k = flat // NT
    live = flat % NT < jnp.repeat(pair_count.reshape(NK), NT)
    row, col = x * NZL + zl, (zh * NY + y) * NCORE + c
    source = (k - row) % NK
    from_zh, from_y, from_c = source // (NY * NCORE), source // NCORE % NY, source % NCORE
    near = from_zh == zh
    part = jnp.where(from_c == 0, jnp.where(near, 0, 1), jnp.where(near, 2, 3))
    left = (jnp.where(c == 1, 0, NY) + seat_of(from_y - y)) * TILE + part * NA + pairs[:, 0]
    holder = (k - col) % NK
    part = (zl - holder % NZL) % NZL
    part = part ^ part // 2
    right = (jnp.where(c == 0, 0, NY) + seat_of(holder // NZL - x)) * TILE
    right = right + (part * NCORE + c) * NB + pairs[:, 1]
    code = left * 512 + right
    target = jnp.arange(NC, dtype=jnp.int32)[:, None]
    mine = live[None] & (pairs[:, 2][None] == target)
    seat = jnp.sum(mine[:, None, :] & (flat[None, None, :] < flat[None, :, None]), axis=-1)
    hit = mine[:, :, None] & (seat[:, :, None] == flat[None, None, :])
    listed = jnp.sum(jnp.where(hit, code[None, :, None] - ZERO, 0), axis=1) + ZERO
    return listed.astype(jnp.int32), jnp.sum(mine, axis=1).astype(jnp.int32)


def product_kernel(plan, codes, counts, *refs):
    pieces, (out, held, sems) = refs[:-3], refs[-3:]
    copies = []
    for piece, (size, at) in zip(pieces, plan, strict=True):
        copies.append(
            pltpu.make_async_copy(piece, held.at[pl.ds(at, size)], sems.at[len(copies)])
        )
    for copy in copies:
        copy.start()
    held[ZERO] = jnp.zeros((BS, BS), jnp.bfloat16)
    for copy in copies:
        copy.wait()

    def part(n, step):
        first, second = [], []
        for g in range(GROUP):
            code = codes[n, step * GROUP + g]
            first.append(held[code // 512])
            second.append(held[code % 512])
        return jnp.dot(
            jnp.concatenate(first, axis=1),
            jnp.concatenate(second, axis=0),
            preferred_element_type=jnp.float32,
        )

    steps = (jnp.maximum(counts[0], counts[1]) + GROUP - 1) // GROUP
    zero = jnp.zeros((BS, BS), jnp.float32)

    def step(turn, total):
        return total[0] + part(0, turn), total[1] + part(1, turn)

    total = lax.fori_loop(0, steps, step, (zero, zero))
    out[0] = total[0].astype(jnp.bfloat16)
    out[1] = total[1].astype(jnp.bfloat16)


def along_plane(value, shift):
    pairs = []
    for x in range(NX):
        for y in range(NY):
            place = (x * NY + y) * NCORE
            pairs.append((place, ((x + shift) % NX * NY + y) * NCORE))
            pairs.append((place + 1, (x * NY + (y + shift) % NY) * NCORE + 1))
    return lax.ppermute(value, ("x", "y", "c"), pairs)


def along_z(value, shift, swap):
    pairs = []
    for zl in range(NZL):
        for zh in range(NZH):
            place = (zl * NZH + zh) * NCORE
            pairs.append((place, ((zl + shift) % NZL * NZH + zh) * NCORE))
            pairs.append((place + 1, (zl * NZH + (zh + swap) % NZH) * NCORE + 1))
    return lax.ppermute(value, ("zl", "zh", "c"), pairs)


def to_partner(value):
    return lax.ppermute(value, "c", rot(NCORE, 1))


def per_device(left_blocks, right_blocks, pair_lists, pair_count):
    x, zl, zh, y, c = (lax.axis_index(name) for name in ("x", "zl", "zh", "y", "c"))

    got = to_partner(jnp.where(c == 0, left_blocks, jnp.concatenate([right_blocks] * 2)))
    rights = jnp.concatenate([right_blocks, got[:NB]])
    first, second = jnp.where(c == 0, rights, got), jnp.where(c == 0, rights, left_blocks)
    own = jnp.concatenate(
        [first, along_z(first, 1, 1), along_z(second, 3, 0), along_z(second, 2, 1)]
    )
    own = lax.optimization_barrier(own)
    half = TILE // 2
    behind, ahead = along_plane(own, 2), along_plane(own, -2)
    near = jnp.concatenate([behind, own, ahead])
    pieces = [own, jnp.concatenate([behind, ahead])]
    pieces += [along_plane(near[: 2 * TILE], 1), along_plane(near[TILE:], -1)]
    far = [along_plane(behind[:half], 2), along_plane(ahead[half:], -2)]
    pieces.append(jnp.concatenate(far))
    pieces += [to_partner(piece) for piece in pieces]
    plan, at = [], 0
    for piece in pieces:
        plan.append((piece.shape[0], at))
        at += piece.shape[0]

    codes, counts = slot_lists(pair_lists, pair_count, x, zl, zh, y, c)

    def kernel(*refs):
        product_kernel(plan, *refs)

    return pl.pallas_call(
        kernel,
        out_shape=jax.ShapeDtypeStruct((NC, BS, BS), jnp.bfloat16),
        in_specs=[pl.BlockSpec(memory_space=pltpu.SMEM)] * 2
        + [pl.BlockSpec(memory_space=pl.ANY)] * len(pieces),
        out_specs=pl.BlockSpec(memory_space=pltpu.VMEM),
        scratch_shapes=[
            pltpu.VMEM((ZERO + 1, BS, BS), jnp.bfloat16),
            pltpu.SemaphoreType.DMA((len(plan),)),
        ],
        compiler_params=pltpu.CompilerParams(vmem_limit_bytes=16 * 1024 * 1024),
        cost_estimate=pl.CostEstimate(
            flops=2 * 128 * BS**3, bytes_accessed=6 * 1024 * 1024, transcendentals=0
        ),
        name="block_products",
    )(codes, counts, *pieces)


def solution(mesh):
    parts = Mesh(mesh.devices.reshape(NX, NZL, NZH, NY, NCORE), ("x", "zl", "zh", "y", "c"))
    row, col = ("x", "zl"), ("zh", "y", "c")
    return jax.shard_map(
        per_device,
        mesh=parts,
        in_specs=(P(row, col, None), P(col, row, None), P(row + col, None, None), P(row + col, None)),
        out_specs=P(row + col, None, None),
        check_vma=False,
    )
```
